256 devices in a mesh: tmpl: 16 (over z, core), sta: 16 (over y, x).
Axes of the slice: x: 4, y: 4, z: 8, core: 2. Of those that a mesh axis runs over, the one named last changes fastest.
Arguments:
- waveforms: float32 [512, 3, 8192], P('sta', None, 'tmpl'), may hold values from -450 to 450
- templates: bfloat16 [512, 128, 450], P('sta', 'tmpl'), may hold values from -40 to 40
- pair_rows: int32 [512, 128], P('sta', 'tmpl'), may hold values from 0 to 4096, as said below
Outputs:
- detection: float32 [4096, 8192], P(('tmpl', 'sta'))
The draws below stay inside these ranges and needn't reach their ends.
Inputs may be any that keep to these rules, and one draw needn't show every extreme that they name: Slot j of template block b at station s is pair_rows[s, b * 8 + j]. In each block the live slots come first and hold detection rows; the rest hold 4096. A block's live count is at most 8, and in every block some station has all 8 slots live. The rows of one station are distinct. A row r has home region (r // 16) % 16, and only stations of regions h - 1, h and h + 1 (taken cyclically, region of station s = s // 32) carry a row of home region h.
All inputs are finite; a program needn't handle non-finite values.
Results may differ from the reference program's by a relative error of at most 0.0065.
Values may be sent and summed in bfloat16 or wider, within the bound.
A program may use at most 64 MiB of HBM per device.

```python
import jax
import jax.numpy as jnp
from jax import lax

STA_DEV = 32
TLEN = 150
CAP = 8
ROWS_DEV = 16
STATIONS = 512
LAGS = 8192
SLOTS = 128
TEMPLATES = 4096


def draw_waveforms(key, part):
    key = jax.random.fold_in(key, 11)
    keys = jax.random.split(key, 3)
    shape = (STATIONS, 3, LAGS)
    base = jnp.clip(jax.random.normal(keys[0], shape, jnp.float32), -4.0, 4.0)
    spread = jnp.log(10.0)
    channel = jnp.exp(jax.random.uniform(keys[1], (STATIONS, 3, 1), jnp.float32, 0.0, 1.0) * spread)
    pieces = jnp.exp(jax.random.uniform(keys[2], (STATIONS, 1, LAGS // 32), jnp.float32, 0.0, 1.0) * spread)
    pieces = jnp.repeat(pieces, 32, axis=2)
    return base * channel * pieces


def draw_templates(key, part):
    key = jax.random.fold_in(key, 23)
    keys = jax.random.split(key, 2)
    shape = (STATIONS, SLOTS, 3, TLEN)
    base = jnp.clip(jax.random.normal(keys[0], shape, jnp.float32), -4.0, 4.0)
    spread = jnp.log(10.0)
    amplitude = jnp.exp(jax.random.uniform(keys[1], (STATIONS, SLOTS, 3, 1), jnp.float32, 0.0, 1.0) * spread)
    return (base * amplitude).reshape(STATIONS, SLOTS, 3 * TLEN).astype(jnp.bfloat16)


def draw_pair_rows(key, part):
    key = jax.random.fold_in(key, 37)
    keys = jax.random.split(key, 3)
    regions = STATIONS // STA_DEV
    blocks = SLOTS // CAP
    row_group = ROWS_DEV * regions
    pool_size = 3 * blocks * ROWS_DEV
    candidates = jnp.broadcast_to(jnp.arange(pool_size, dtype=jnp.int32), (STATIONS, pool_size))
    chosen = jax.random.permutation(keys[0], candidates, axis=1, independent=True)[:, :SLOTS]
    relative = chosen % 3
    remainder = chosen // 3
    group_id = remainder // ROWS_DEV
    within = remainder % ROWS_DEV
    station_region = jnp.arange(STATIONS, dtype=jnp.int32) // STA_DEV
    home_region = (station_region[:, None] + relative - 1 + regions) % regions
    row_value = group_id * row_group + home_region * ROWS_DEV + within
    counts = jax.random.randint(keys[1], (STATIONS, blocks), 0, CAP + 1)
    fullest = jax.random.randint(keys[2], (blocks,), 0, STATIONS)
    counts = jnp.where(jnp.arange(STATIONS, dtype=jnp.int32)[:, None] == fullest[None, :], CAP, counts)
    slot_ids = jnp.arange(SLOTS, dtype=jnp.int32)
    occupied = (slot_ids % CAP)[None, :] < counts[:, slot_ids // CAP]
    return jnp.where(occupied, row_value, TEMPLATES).astype(jnp.int32)


def setup_inputs(seed: int = 0) -> dict:
    key_of = jax.random.split(jax.random.key(seed), 4)
    waveforms = draw_waveforms(jax.random.fold_in(key_of[3], 71), 0)
    templates = draw_templates(jax.random.fold_in(key_of[3], 71), 0)
    pair_rows = draw_pair_rows(jax.random.fold_in(key_of[3], 71), 0)
    return dict(waveforms=waveforms, templates=templates, pair_rows=pair_rows)


def reference(waveforms, templates, pair_rows):
    window_size = 3 * TLEN
    station_span = 8
    coarse = lax.optimization_barrier(waveforms.astype(jnp.bfloat16)).astype(jnp.float32)
    extended = jnp.concatenate([coarse, jnp.zeros((STATIONS, 3, TLEN - 1), jnp.float32)], axis=2)

    def station_step(position, running):
        offset = position * station_span
        segment = lax.dynamic_slice_in_dim(extended, offset, station_span, 0)
        hankel = jnp.stack([segment[:, :, sample:sample + LAGS] for sample in range(TLEN)], axis=2)
        hankel = hankel.reshape(station_span, window_size, LAGS)
        energy = lax.optimization_barrier(jnp.sum(hankel * hankel, axis=1)) / window_size
        data_scale = lax.rsqrt(energy + 1e-06)
        template_set = lax.dynamic_slice_in_dim(templates, offset, station_span, 0).astype(jnp.float32)
        wave_scale = lax.rsqrt(lax.optimization_barrier(jnp.mean(template_set * template_set, axis=2)) + 1e-06)
        product = jnp.einsum('spk,skl->spl', template_set, hankel, precision=lax.Precision.HIGHEST)
        correlation = product * (wave_scale / window_size)[:, :, None] * data_scale[:, None, :]
        row_ids = lax.dynamic_slice_in_dim(pair_rows, offset, station_span, 0).reshape(-1)
        return running.at[row_ids].add(correlation.reshape(-1, LAGS), mode='drop')
    return lax.fori_loop(0, STATIONS // station_span, station_step, jnp.zeros((TEMPLATES, LAGS), jnp.float32))
```

```python
import functools

import jax
import jax.numpy as jnp
from jax import lax
from jax.experimental import pallas as pl
from jax.experimental.pallas import tpu as pltpu
from jax.sharding import PartitionSpec as P

TLEN = 150
WINDOW = 450
EPS = 1e-06
CAP = 8
ROWS_DEV = 16
STATIONS = 32
HALF = 16
LAGS = 512
WIDE = 768
DEPTH = 512
SLOTS = 128
CHUNKS = 8
SPAN = HALF // CHUNKS
CHIPS = 8
BLOCKS = 16
REGIONS = 16
FAR = 4
PIECES = 4
PIECE = 256 // PIECES
MESH = pl.DeviceIdType.MESH


def kernel(
    waves_ref, own_ref, out_ref,
    bank, hankel, shifts, wave, mate, halo_out, halo_in, scale_ref, corr, rows_ref, total,
    outgo, income, part, gathered,
    mate_sem, halo_sem, ring_send, ring_recv, share_send, share_recv, side_send, side_recv,
    spread_send, spread_recv,
):
    block = lax.axis_index("tmpl")
    region = lax.axis_index("sta")
    z = block // 2
    core = block % 2
    other = 1 - core

    def at(chip, which):
        return (lax.rem(chip + CHIPS, CHIPS) * 2 + which, region)

    barrier = pltpu.get_barrier_semaphore()

    @pl.loop(1, BLOCKS)
    def _(step):
        pl.semaphore_signal(
            barrier, inc=1, device_id=(lax.rem(block + step, BLOCKS), region), device_id_type=MESH
        )

    for side in (1, REGIONS - 1):
        pl.semaphore_signal(
            barrier, inc=1, device_id=(block, lax.rem(region + side, REGIONS)), device_id_type=MESH
        )

    coarse = waves_ref[...].astype(jnp.bfloat16)
    halo_out[...] = coarse[:, :256]
    for tile in range(4):
        wave[tile] = coarse[:, tile * 128 : tile * 128 + 128].astype(jnp.float32)
    pl.semaphore_wait(barrier, BLOCKS + 1)

    to_mate = pltpu.make_async_remote_copy(
        src_ref=own_ref.at[pl.ds(pl.multiple_of(other * 128, 128), 128)],
        dst_ref=mate,
        send_sem=mate_sem.at[0],
        recv_sem=mate_sem.at[1],
        device_id=at(z, other),
        device_id_type=MESH,
    )
    to_mate.start()
    to_left = pltpu.make_async_remote_copy(
        src_ref=halo_out,
        dst_ref=halo_in,
        send_sem=halo_sem.at[0],
        recv_sem=halo_sem.at[1],
        device_id=(lax.rem(block + BLOCKS - 1, BLOCKS), region),
        device_id_type=MESH,
    )
    to_left.start()

    total[...] = jnp.zeros_like(total)

    def place(who, chunk, chip):
        first = pl.multiple_of(who * HALF + chunk * SPAN, SPAN)
        chip = lax.rem(chip + CHIPS, CHIPS)
        return bank.at[pl.ds(first, SPAN), pl.ds(pl.multiple_of(chip * 16, 16), 16), :]

    def ring(way, chunk, hop, origin):
        ref = place(core, chunk, origin)
        return pltpu.make_async_remote_copy(
            src_ref=ref,
            dst_ref=ref,
            send_sem=ring_send.at[way, chunk, hop],
            recv_sem=ring_recv.at[way, chunk, hop],
            device_id=at(z + (1 if way == 0 else -1), core),
            device_id_type=MESH,
        )

    def share(who, chunk, away, chip):
        ref = place(who, chunk, chip)
        return pltpu.make_async_remote_copy(
            src_ref=ref,
            dst_ref=ref,
            send_sem=share_send.at[chunk, away],
            recv_sem=share_recv.at[chunk, away],
            device_id=at(z, other),
            device_id_type=MESH,
        )

    to_mate.wait()
    for pair in range(HALF // 2):
        mine = own_ref[pl.ds(pl.multiple_of(core * 128 + pair * 16, 16), 16), :].astype(jnp.float32)
        theirs = mate[pl.ds(pair * 16, 16), :].astype(jnp.float32)
        low = jnp.where(core == 0, mine, theirs)
        high = jnp.where(core == 0, theirs, mine)
        for i in range(2):
            both = jnp.concatenate([low[8 * i : 8 * i + 8], high[8 * i : 8 * i + 8]], axis=0)
            bank[core * HALF + pair * 2 + i, pl.ds(pl.multiple_of(z * 16, 16), 16), :] = both.astype(
                jnp.bfloat16
            )

    def waves_ready():
        to_left.wait()
        last = jnp.where(block == BLOCKS - 1, 0.0, 1.0)
        for tile in range(2):
            one = halo_in[:, tile * 128 : tile * 128 + 128]
            wave[4 + tile] = one.astype(jnp.float32) * last
        every = jnp.concatenate([wave[tile] for tile in range(6)], axis=1)
        for lane in range(16):
            moved = every if lane == 0 else pltpu.roll(every, WIDE - lane, 1)
            for tile in range(6):
                shifts[tile, pl.ds(lane, 96, stride=16), :] = moved[:, tile * 128 : tile * 128 + 128]
        pieces = []
        for tile in range(6):
            squared = jnp.zeros((STATIONS, 128), jnp.float32)
            for channel in range(3):
                one = wave[tile, pl.ds(channel, STATIONS, stride=3), :]
                squared = squared + one * one
            pieces.append(squared)
        squared = jnp.concatenate(pieces, axis=1)
        def left(x, by):
            return pltpu.roll(x, WIDE - by, 1)
        two = squared + left(squared, 1)
        four = two + left(two, 2)
        run = four
        for by in (4, 8):
            run = run + left(run, by)
        sixteen = run
        for by in (16, 32, 64):
            run = run + left(run, by)
        run = run + left(sixteen, 128) + left(four, 144) + left(two, 148)
        scale_ref[...] = lax.rsqrt(run[:, :LAGS] / WINDOW + EPS)

    lower = lax.broadcasted_iota(jnp.int32, (16, LAGS), 0)

    def build(station):
        rolled = []
        for c in range(3):
            rows = pl.ds(pl.multiple_of((station * 3 + c) * 16, 16), 16)
            every = jnp.concatenate([shifts[tile, rows, :] for tile in range(6)], axis=1)
            rolled.append(every.astype(jnp.bfloat16))

        def taken(channel, start):
            if start >= 0:
                return rolled[channel][:, start : start + LAGS]
            return pltpu.roll(rolled[channel].astype(jnp.float32), -start, 1)[:, :LAGS].astype(jnp.bfloat16)

        for tile in range(DEPTH // 16):
            first = tile * 16
            if first >= WINDOW:
                value = jnp.zeros((16, LAGS), jnp.bfloat16)
            else:
                channel, start = divmod(first, TLEN)
                value = taken(channel, start)
                rest = TLEN - start
                if rest < 16:
                    if channel < 2:
                        after = taken(channel + 1, start - TLEN)
                    else:
                        after = jnp.zeros((16, LAGS), jnp.bfloat16)
                    value = jnp.where(lower < rest, value, after)
            hankel[station, pl.ds(first, 16), :] = value

    ids = lax.broadcasted_iota(jnp.int32, (16, SLOTS), 1)
    picker = jnp.where(ids == WINDOW - 384, 64.0, jnp.where(ids == WINDOW + 1 - 384, 1.0, 0.0))
    picker = picker.astype(jnp.bfloat16)
    live = lax.broadcasted_iota(jnp.int32, (SLOTS, DEPTH), 1) < WINDOW

    def correlate(station, where):
        waves = bank[station]
        product = jnp.dot(waves, hankel[station], preferred_element_type=jnp.float32)
        wide = jnp.where(live, waves.astype(jnp.float32), 0.0)
        power = jnp.sum(wide * wide, axis=1, keepdims=True)
        factor = lax.rsqrt(power / WINDOW + EPS) / WINDOW
        value = product * factor * scale_ref[pl.ds(station, 1), :]
        start = pl.multiple_of(where * SLOTS, SLOTS)
        corr[pl.ds(start, SLOTS), :] = value.astype(jnp.bfloat16)
        row = lax.dot_general(
            picker, waves[:, 384:], (((1,), (1,)), ((), ())), preferred_element_type=jnp.float32
        )
        row = row[:8].astype(jnp.int32)
        group = row >> 8
        home = (row >> 4) & 15
        relative = (home - region + 1 + REGIONS) & 15
        apart = ((group >> 1) - z + CHIPS) & 7
        order = jnp.where(apart >= 4, 2 * apart - 8, 7 - 2 * apart)
        index = relative * 256 + (order * 2 + (group & 1)) * ROWS_DEV + (row & 15)
        index = jnp.where(row < 4096, index, 4096)
        rows_ref[where] = index

    across = lax.broadcasted_iota(jnp.int32, (256, SLOTS), 0)

    def scatter(relative):
        picks = []
        for i in range(2 * SPAN):
            index = rows_ref[i][:1, :]
            picks.append((across + relative * 256 == index).astype(jnp.bfloat16))
        selector = jnp.concatenate(picks, axis=1)
        start = pl.multiple_of(relative * 256, 256)
        total[pl.ds(start, 256), :] += jnp.dot(
            selector, corr[...], preferred_element_type=jnp.float32
        )

    def hops_of(way):
        return range(FAR)

    def moves(turn):
        for hop in range(FAR):
            chunk = turn - 1 - hop
            inside = (chunk >= 0) & (chunk < CHUNKS)
            for way in range(2):
                sign = -1 if way == 0 else 1
                arrives = inside
                if hop == FAR - 1:
                    arrives = inside & (lax.rem(chunk + CHUNKS, 2) == way)

                @pl.when(arrives)
                def _():
                    origin = z + sign * (hop + 1)
                    ring(way, chunk, hop, origin).wait_recv()
                    away = hop + 1 if way == 0 else CHIPS - 1 - hop
                    if hop + 1 < FAR - 1:
                        ring(way, chunk, hop + 1, origin).start()
                    elif hop + 1 == FAR - 1:

                        @pl.when(lax.rem(chunk, 2) == way)
                        def _():
                            ring(way, chunk, hop + 1, origin).start()

                    share(core, chunk, away, origin).start()

        @pl.when(turn < CHUNKS)
        def _():
            for way in range(2):
                ring(way, turn, 0, z).start()
            share(core, turn, 0, z).start()

    @pl.loop(0, CHUNKS + FAR)
    def _(turn):
        moves(turn)

        @pl.when(turn == 0)
        def _():
            waves_ready()

        @pl.when(turn < FAR)
        def _():
            @pl.loop(0, STATIONS // FAR)
            def _(i):
                build(turn * (STATIONS // FAR) + i)

        @pl.when(turn >= FAR)
        def _():
            chunk = turn - FAR

            @pl.loop(0, SPAN)
            def _(i):
                correlate(core * HALF + chunk * SPAN + i, i)

            @pl.loop(0, CHIPS)
            def _(away):
                share(other, chunk, away, z).wait_recv()

            @pl.loop(0, SPAN)
            def _(i):
                correlate(other * HALF + chunk * SPAN + i, SPAN + i)

            @pl.when(turn < CHUNKS + FAR - 1)
            def _():
                @pl.loop(0, 3)
                def _(relative):
                    scatter(relative)

    def side(direction, piece):
        step = REGIONS - 1 if direction == 0 else 1
        span = pl.ds(piece * PIECE, PIECE)
        return pltpu.make_async_remote_copy(
            src_ref=outgo.at[direction, span],
            dst_ref=income.at[direction, span],
            send_sem=side_send.at[direction, piece],
            recv_sem=side_recv.at[direction, piece],
            device_id=(block, lax.rem(region + step, REGIONS)),
            device_id_type=MESH,
        )

    for direction in range(2):
        scatter(2 * direction)
        outgo[direction] = total[pl.ds(512 * direction, 256), :].astype(jnp.bfloat16)
        for piece in range(PIECES):
            side(direction, piece).start()
    scatter(1)

    def spread(piece, slot):
        order = piece * 2 + slot // 2
        apart = 4 + order // 2 if order % 2 == 0 else 3 - order // 2
        return order, apart, slot % 2

    def send_out(order, apart, which):
        rows = pl.ds((order * 2 + which) * ROWS_DEV, ROWS_DEV)
        return pltpu.make_async_remote_copy(
            src_ref=part.at[rows],
            dst_ref=gathered.at[block],
            send_sem=spread_send.at[order * 2 + which],
            recv_sem=spread_recv.at[block],
            device_id=at(z + apart, which),
            device_id_type=MESH,
        )

    for piece in range(PIECES):
        for direction in range(2):
            side(direction, piece).wait_recv()
        span = pl.ds(piece * PIECE, PIECE)
        summed = total[pl.ds(256 + piece * PIECE, PIECE), :]
        summed = summed + income[0, span].astype(jnp.float32) + income[1, span].astype(jnp.float32)
        part[span] = summed.astype(jnp.bfloat16)
        for slot in range(4):
            order, apart, which = spread(piece, slot)
            if apart == 0:

                @pl.when(core != which)
                def _():
                    send_out(order, apart, which).start()

            else:
                send_out(order, apart, which).start()

    here = pl.ds(pl.multiple_of((14 + core) * ROWS_DEV, ROWS_DEV), ROWS_DEV)
    gathered[block] = part[here]

    @pl.loop(0, CHUNKS)
    def _(chunk):
        for way in range(2):
            for hop in range(FAR - 1):
                ring(way, chunk, hop, z).wait_send()

            @pl.when(lax.rem(chunk, 2) == way)
            def _():
                ring(way, chunk, FAR - 1, z).wait_send()

        @pl.loop(0, CHIPS)
        def _(away):
            share(core, chunk, away, z).wait_send()

    for direction in range(2):
        for piece in range(PIECES):
            side(direction, piece).wait_send()

    def spread_wait(source):
        return pltpu.make_async_remote_copy(
            src_ref=part.at[pl.ds(0, ROWS_DEV)],
            dst_ref=gathered.at[source],
            send_sem=spread_send.at[0],
            recv_sem=spread_recv.at[source],
            device_id=(block, region),
            device_id_type=MESH,
        )

    for piece in range(PIECES):
        for slot in range(4):
            order, apart, which = spread(piece, slot)
            if apart == 0:

                @pl.when(core != which)
                def _():
                    send_out(order, apart, which).wait_send()

            else:
                send_out(order, apart, which).wait_send()

    @pl.loop(1, BLOCKS)
    def _(step):
        spread_wait(lax.rem(block + step, BLOCKS)).wait_recv()

    for source in range(BLOCKS):
        out_ref[:, pl.ds(source * LAGS, LAGS)] = gathered[source]


def on_device(waveforms, templates, pair_rows):
    waves = waveforms.reshape(STATIONS * 3, LAGS)
    number = jnp.stack([pair_rows >> 6, pair_rows & 63], axis=2).astype(jnp.bfloat16)
    fill = jnp.zeros((STATIONS, CAP, DEPTH - WINDOW - 2), jnp.bfloat16)
    own = jnp.concatenate([templates, number, fill], axis=2).reshape(STATIONS * CAP, DEPTH)
    bf16, f32 = jnp.bfloat16, jnp.float32
    dma = pltpu.SemaphoreType.DMA
    result = pl.pallas_call(
        kernel,
        out_shape=jax.ShapeDtypeStruct((ROWS_DEV, BLOCKS * LAGS), bf16),
        in_specs=[pl.BlockSpec(memory_space=pltpu.VMEM)] * 2,
        out_specs=pl.BlockSpec(memory_space=pltpu.VMEM),
        scratch_shapes=[
            pltpu.VMEM((STATIONS, SLOTS, DEPTH), bf16),
            pltpu.VMEM((STATIONS, DEPTH, LAGS), bf16),
            pltpu.VMEM((6, STATIONS * 3 * 16, 128), f32),
            pltpu.VMEM((6, STATIONS * 3, 128), f32),
            pltpu.VMEM((128, DEPTH), bf16),
            pltpu.VMEM((STATIONS * 3, 256), bf16),
            pltpu.VMEM((STATIONS * 3, 256), bf16),
            pltpu.VMEM((STATIONS, LAGS), f32),
            pltpu.VMEM((2 * SPAN * SLOTS, LAGS), bf16),
            pltpu.VMEM((2 * SPAN, 8, SLOTS), jnp.int32),
            pltpu.VMEM((768, LAGS), f32),
            pltpu.VMEM((2, 256, LAGS), bf16),
            pltpu.VMEM((2, 256, LAGS), bf16),
            pltpu.VMEM((256, LAGS), bf16),
            pltpu.VMEM((BLOCKS, ROWS_DEV, LAGS), bf16),
            dma((2,)),
            dma((2,)),
            dma((2, CHUNKS, FAR)),
            dma((2, CHUNKS, FAR)),
            dma((CHUNKS, CHIPS)),
            dma((CHUNKS, CHIPS)),
            dma((2, PIECES)),
            dma((2, PIECES)),
            dma((BLOCKS,)),
            dma((BLOCKS,)),
        ],
        compiler_params=pltpu.CompilerParams(
            collective_id=0, has_side_effects=True, vmem_limit_bytes=60 * 1024 * 1024
        ),
    )(waves, own)
    return result.astype(jnp.float32)


def solution(mesh):
    in_specs = (P("sta", None, "tmpl"), P("sta", "tmpl", None), P("sta", "tmpl"))
    out_specs = P(("tmpl", "sta"), None)
    return jax.shard_map(
        on_device, mesh=mesh, in_specs=in_specs, out_specs=out_specs, check_vma=False
    )
```

```python
import functools

import jax
import jax.numpy as jnp
from jax import lax
from jax.experimental import pallas as pl
from jax.experimental.pallas import tpu as pltpu
from jax.sharding import PartitionSpec as P

TLEN = 150
WINDOW = 450
EPS = 1e-06
CAP = 8
ROWS_DEV = 16
STATIONS = 32
LAGS = 512
WIDE = 768
DEPTH = 512
SLOTS = 128
CHUNKS = 8
SPAN = STATIONS // CHUNKS
AHEAD = 3
CHIPS = 8
BLOCKS = 16
REGIONS = 16
FAR = 4
PIECES = 4
PIECE = 256 // PIECES
MESH = pl.DeviceIdType.MESH


def kernel(
    waves_ref, own_ref, number_ref, out_ref,
    bank, hankel, shifts, wave, halo_out, halo_in, scale_ref, corr, rows_ref, total,
    outgo, income, part, gathered,
    halo_sem, ring_send, ring_recv, share_send, share_recv, side_send, side_recv,
    spread_send, spread_recv,
):
    block = lax.axis_index("tmpl")
    region = lax.axis_index("sta")
    z = block // 2
    core = block % 2
    other = 1 - core

    def at(chip, which):
        return (lax.rem(chip + CHIPS, CHIPS) * 2 + which, region)

    barrier = pltpu.get_barrier_semaphore()
    near = [at(z, other), at(z + 1, core), at(z - 1, core), at(z + 2 * core - 1, other)]
    near += [(block, lax.rem(region + side, REGIONS)) for side in (1, REGIONS - 1)]
    for device in near:
        pl.semaphore_signal(barrier, inc=1, device_id=device, device_id_type=MESH)

    coarse = waves_ref[...].astype(jnp.bfloat16)
    halo_out[...] = coarse[:, :256]
    for tile in range(4):
        wave[tile] = coarse[:, tile * 128 : tile * 128 + 128].astype(jnp.float32)

    station = lax.broadcasted_iota(jnp.int32, (STATIONS * CAP, STATIONS), 0) >> 3
    expand = (station == lax.broadcasted_iota(jnp.int32, (STATIONS * CAP, STATIONS), 1))
    expand = expand.astype(jnp.bfloat16)
    mine = lax.broadcasted_iota(jnp.int32, (STATIONS * CAP, CAP), 0) & 7
    mine = mine == lax.broadcasted_iota(jnp.int32, (STATIONS * CAP, CAP), 1)
    lane = lax.broadcasted_iota(jnp.int32, (STATIONS * CAP, 128), 1)
    numbers = jnp.zeros((STATIONS * CAP, 128), jnp.float32)
    for i, digits in enumerate((number_ref[...] >> 6, number_ref[...] & 63)):
        digits = digits.astype(jnp.float32).astype(jnp.bfloat16)
        column = jnp.dot(expand, digits, preferred_element_type=jnp.float32)
        column = jnp.sum(jnp.where(mine, column, 0.0), axis=1, keepdims=True)
        numbers = jnp.where(lane == WINDOW - 384 + i, column, numbers)
    bank[block, :, :384] = own_ref[:, :384]
    bank[block, :, 384:] = numbers.astype(jnp.bfloat16)
    bank[block, :, 384:WINDOW] = own_ref[:, 384:]
    pl.semaphore_wait(barrier, len(near))

    to_left = pltpu.make_async_remote_copy(
        src_ref=halo_out,
        dst_ref=halo_in,
        send_sem=halo_sem.at[0],
        recv_sem=halo_sem.at[1],
        device_id=(lax.rem(block + BLOCKS - 1, BLOCKS), region),
        device_id_type=MESH,
    )
    to_left.start()

    def place(chunk, chip, which):
        first = pl.multiple_of(chunk * SPAN * CAP, SPAN * CAP)
        return bank.at[lax.rem(chip + CHIPS, CHIPS) * 2 + which, pl.ds(first, SPAN * CAP), :]

    def ring(way, chunk, hop, origin):
        ref = place(chunk, origin, core)
        return pltpu.make_async_remote_copy(
            src_ref=ref,
            dst_ref=ref,
            send_sem=ring_send,
            recv_sem=ring_recv.at[way, chunk, hop],
            device_id=at(z + (1 if way == 0 else -1), core),
            device_id_type=MESH,
        )

    def share(chunk, chip):
        ref = place(chunk, chip, core)
        return pltpu.make_async_remote_copy(
            src_ref=ref,
            dst_ref=ref,
            send_sem=share_send,
            recv_sem=share_recv.at[chunk],
            device_id=at(z, other),
            device_id_type=MESH,
        )

    def bulk(count, send, receive):
        ref = bank.at[pl.ds(0, count // CHUNKS)]
        return pltpu.make_async_remote_copy(
            src_ref=ref, dst_ref=ref, send_sem=send, recv_sem=receive,
            device_id=at(z, other), device_id_type=MESH,
        )

    def inject(chunk):
        for way in range(2):
            ring(way, chunk, 0, z).start()
        share(chunk, z).start()

    for chunk in range(AHEAD + 1):
        inject(chunk)

    total[...] = jnp.zeros_like(total)

    def waves_ready():
        to_left.wait()
        last = jnp.where(block == BLOCKS - 1, 0.0, 1.0)
        for tile in range(2):
            one = halo_in[:, tile * 128 : tile * 128 + 128]
            wave[4 + tile] = one.astype(jnp.float32) * last
        every = jnp.concatenate([wave[tile] for tile in range(6)], axis=1)
        for lane in range(16):
            moved = every if lane == 0 else pltpu.roll(every, WIDE - lane, 1)
            for tile in range(6):
                shifts[tile, pl.ds(lane, 96, stride=16), :] = moved[:, tile * 128 : tile * 128 + 128]
        pieces = []
        for tile in range(6):
            squared = jnp.zeros((STATIONS, 128), jnp.float32)
            for channel in range(3):
                one = wave[tile, pl.ds(channel, STATIONS, stride=3), :]
                squared = squared + one * one
            pieces.append(squared)
        squared = jnp.concatenate(pieces, axis=1)
        def left(x, by):
            return pltpu.roll(x, WIDE - by, 1)
        two = squared + left(squared, 1)
        four = two + left(two, 2)
        run = four
        for by in (4, 8):
            run = run + left(run, by)
        sixteen = run
        for by in (16, 32, 64):
            run = run + left(run, by)
        run = run + left(sixteen, 128) + left(four, 144) + left(two, 148)
        scale_ref[...] = lax.rsqrt(run[:, :LAGS] / WINDOW + EPS)

    lower = lax.broadcasted_iota(jnp.int32, (16, LAGS), 0)

    def build(station):
        rolled = []
        for c in range(3):
            rows = pl.ds(pl.multiple_of((station * 3 + c) * 16, 16), 16)
            rolled.append(jnp.concatenate([shifts[tile, rows, :] for tile in range(6)], axis=1))

        def taken(channel, start):
            if start == 0:
                return rolled[channel][:, :LAGS]
            return pltpu.roll(rolled[channel], (WIDE - start) % WIDE, 1)[:, :LAGS]

        for tile in range(DEPTH // 16):
            first = tile * 16
            if first >= WINDOW:
                value = jnp.zeros((16, LAGS), jnp.float32)
            else:
                channel, start = divmod(first, TLEN)
                value = taken(channel, start)
                rest = TLEN - start
                if rest < 16:
                    if channel < 2:
                        after = taken(channel + 1, start - TLEN)
                    else:
                        after = jnp.zeros((16, LAGS), jnp.float32)
                    value = jnp.where(lower < rest, value, after)
            hankel[station, pl.ds(first, 16), :] = value.astype(jnp.bfloat16)

    ids = lax.broadcasted_iota(jnp.int32, (16, SLOTS), 1)
    picker = jnp.where(ids == WINDOW - 384, 64.0, jnp.where(ids == WINDOW + 1 - 384, 1.0, 0.0))
    picker = picker.astype(jnp.bfloat16)
    live = lax.broadcasted_iota(jnp.int32, (SLOTS, 128), 1) < WINDOW - 384

    def correlate(pair, where):
        rows = pl.ds(pl.multiple_of(pair * 16, 16), 16)
        both = [bank[b, rows, :].astype(jnp.float32) for b in range(BLOCKS)]
        for i in range(2):
            one(pair * 2 + i, where * 2 + i, [x[i * 8 : i * 8 + 8] for x in both])

    def one(station, where, pieces):
        wide = jnp.concatenate(pieces, axis=0)
        waves = wide.astype(jnp.bfloat16)
        product = jnp.dot(waves, hankel[station], preferred_element_type=jnp.float32)
        last = jnp.where(live, wide[:, 384:], 0.0)
        power = last * last
        for tile in range(3):
            power = power + wide[:, tile * 128 : tile * 128 + 128] * wide[:, tile * 128 : tile * 128 + 128]
        power = jnp.sum(power, axis=1, keepdims=True)
        factor = lax.rsqrt(power / WINDOW + EPS) / WINDOW
        value = product * factor * scale_ref[pl.ds(station, 1), :]
        start = pl.multiple_of(where * SLOTS, SLOTS)
        corr[pl.ds(start, SLOTS), :] = value.astype(jnp.bfloat16)
        row = lax.dot_general(
            picker, waves[:, 384:], (((1,), (1,)), ((), ())), preferred_element_type=jnp.float32
        )
        row = row[:8].astype(jnp.int32)
        group = row >> 8
        home = (row >> 4) & 15
        relative = (home - region + 1 + REGIONS) & 15
        apart = ((group >> 1) - z + CHIPS) & 7
        order = jnp.where(apart >= 4, 2 * apart - 8, 7 - 2 * apart)
        index = relative * 256 + (order * 2 + (group & 1)) * ROWS_DEV + (row & 15)
        index = jnp.where(row < 4096, index, 4096)
        rows_ref[where] = index

    across = lax.broadcasted_iota(jnp.int32, (256, SLOTS), 0)

    def scatter(relative):
        picks = []
        for i in range(SPAN):
            index = rows_ref[i][:1, :]
            picks.append((across + relative * 256 == index).astype(jnp.bfloat16))
        selector = jnp.concatenate(picks, axis=1)
        start = pl.multiple_of(relative * 256, 256)
        total[pl.ds(start, 256), :] += jnp.dot(
            selector, corr[...], preferred_element_type=jnp.float32
        )

    def moves(turn):
        for hop in range(FAR):
            chunk = turn - 1 - hop
            inside = (chunk >= 0) & (chunk < CHUNKS)
            for way in range(2):
                sign = -1 if way == 0 else 1
                arrives = inside
                if hop == FAR - 1:
                    arrives = inside & (lax.rem(chunk + CHUNKS, 2) == way)

                @pl.when(arrives)
                def _():
                    origin = z + sign * (hop + 1)
                    ring(way, chunk, hop, origin).wait_recv()
                    if hop + 1 < FAR - 1:
                        ring(way, chunk, hop + 1, origin).start()
                    elif hop + 1 == FAR - 1:

                        @pl.when(lax.rem(chunk, 2) == way)
                        def _():
                            ring(way, chunk, hop + 1, origin).start()

                    share(chunk, origin).start()

        @pl.when((turn >= 1) & (turn + AHEAD < CHUNKS))
        def _():
            inject(turn + AHEAD)

    def spots(chunk):
        @pl.loop(0, SPAN // 2)
        def _(i):
            correlate(chunk * (SPAN // 2) + i, i)

    @pl.loop(0, CHUNKS + FAR)
    def _(turn):
        moves(turn)

        @pl.when(turn == 0)
        def _():
            waves_ready()

        @pl.when(turn < FAR)
        def _():
            @pl.loop(0, STATIONS // FAR)
            def _(i):
                build(turn * (STATIONS // FAR) + i)

        @pl.when(turn > FAR)
        def _():
            @pl.loop(0, 3)
            def _(relative):
                scatter(relative)

        @pl.when(turn >= FAR)
        def _():
            chunk = turn - FAR
            bulk(CHUNKS, share_send, share_recv.at[chunk]).wait_recv()
            spots(chunk)

    def side(direction, piece):
        step = REGIONS - 1 if direction == 0 else 1
        span = pl.ds(piece * PIECE, PIECE)
        return pltpu.make_async_remote_copy(
            src_ref=outgo.at[direction, span],
            dst_ref=income.at[direction, span],
            send_sem=side_send.at[direction, piece],
            recv_sem=side_recv.at[direction, piece],
            device_id=(block, lax.rem(region + step, REGIONS)),
            device_id_type=MESH,
        )

    for direction in range(2):
        scatter(2 * direction)
        outgo[direction] = total[pl.ds(512 * direction, 256), :].astype(jnp.bfloat16)
        for piece in range(PIECES):
            side(direction, piece).start()
    scatter(1)

    def spread(piece, slot):
        order = piece * 2 + slot // 2
        apart = 4 + order // 2 if order % 2 == 0 else 3 - order // 2
        return order, apart, slot % 2

    def send_out(order, apart, which):
        rows = pl.ds((order * 2 + which) * ROWS_DEV, ROWS_DEV)
        return pltpu.make_async_remote_copy(
            src_ref=part.at[rows],
            dst_ref=gathered.at[block],
            send_sem=spread_send.at[order * 2 + which],
            recv_sem=spread_recv.at[block],
            device_id=at(z + apart, which),
            device_id_type=MESH,
        )

    for piece in range(PIECES):
        for direction in range(2):
            side(direction, piece).wait_recv()
        span = pl.ds(piece * PIECE, PIECE)
        summed = total[pl.ds(256 + piece * PIECE, PIECE), :]
        summed = summed + income[0, span].astype(jnp.float32) + income[1, span].astype(jnp.float32)
        part[span] = summed.astype(jnp.bfloat16)
        for slot in range(4):
            order, apart, which = spread(piece, slot)
            if apart == 0:

                @pl.when(core != which)
                def _():
                    send_out(order, apart, which).start()

            else:
                send_out(order, apart, which).start()

    here = pl.ds(pl.multiple_of((14 + core) * ROWS_DEV, ROWS_DEV), ROWS_DEV)
    gathered[block] = part[here]

    bulk(CHUNKS * 7, ring_send, share_recv.at[0]).wait_send()
    bulk(CHUNKS * 8, share_send, share_recv.at[0]).wait_send()
    for direction in range(2):
        for piece in range(PIECES):
            side(direction, piece).wait_send()

    def spread_wait(source):
        return pltpu.make_async_remote_copy(
            src_ref=part.at[pl.ds(0, ROWS_DEV)],
            dst_ref=gathered.at[source],
            send_sem=spread_send.at[0],
            recv_sem=spread_recv.at[source],
            device_id=(block, region),
            device_id_type=MESH,
        )

    for piece in range(PIECES):
        for slot in range(4):
            order, apart, which = spread(piece, slot)
            if apart == 0:

                @pl.when(core != which)
                def _():
                    send_out(order, apart, which).wait_send()

            else:
                send_out(order, apart, which).wait_send()

    @pl.loop(1, BLOCKS)
    def _(step):
        spread_wait(lax.rem(block + step, BLOCKS)).wait_recv()

    for source in range(BLOCKS):
        out_ref[:, pl.ds(source * LAGS, LAGS)] = gathered[source]


def on_device(waveforms, templates, pair_rows):
    waves = waveforms.reshape(STATIONS * 3, LAGS)
    own = templates.reshape(STATIONS * CAP, WINDOW)
    bf16, f32 = jnp.bfloat16, jnp.float32
    dma = pltpu.SemaphoreType.DMA
    result = pl.pallas_call(
        kernel,
        out_shape=jax.ShapeDtypeStruct((ROWS_DEV, BLOCKS * LAGS), bf16),
        in_specs=[pl.BlockSpec(memory_space=pltpu.VMEM)] * 3,
        out_specs=pl.BlockSpec(memory_space=pltpu.VMEM),
        scratch_shapes=[
            pltpu.VMEM((BLOCKS, STATIONS * CAP, DEPTH), bf16),
            pltpu.VMEM((STATIONS, DEPTH, LAGS), bf16),
            pltpu.VMEM((6, STATIONS * 3 * 16, 128), f32),
            pltpu.VMEM((6, STATIONS * 3, 128), f32),
            pltpu.VMEM((STATIONS * 3, 256), bf16),
            pltpu.VMEM((STATIONS * 3, 256), bf16),
            pltpu.VMEM((STATIONS, LAGS), f32),
            pltpu.VMEM((SPAN * SLOTS, LAGS), bf16),
            pltpu.VMEM((SPAN, 8, SLOTS), jnp.int32),
            pltpu.VMEM((768, LAGS), f32),
            pltpu.VMEM((2, 256, LAGS), bf16),
            pltpu.VMEM((2, 256, LAGS), bf16),
            pltpu.VMEM((256, LAGS), bf16),
            pltpu.VMEM((BLOCKS, ROWS_DEV, LAGS), bf16),
            dma((2,)),
            dma,
            dma((2, CHUNKS, FAR)),
            dma,
            dma((CHUNKS,)),
            dma((2, PIECES)),
            dma((2, PIECES)),
            dma((BLOCKS,)),
            dma((BLOCKS,)),
        ],
        compiler_params=pltpu.CompilerParams(
            collective_id=0, has_side_effects=True, vmem_limit_bytes=60 * 1024 * 1024
        ),
    )(waves, own, pair_rows)
    return result.astype(jnp.float32)


def solution(mesh):
    in_specs = (P("sta", None, "tmpl"), P("sta", "tmpl", None), P("sta", "tmpl"))
    out_specs = P(("tmpl", "sta"), None)
    return jax.shard_map(
        on_device, mesh=mesh, in_specs=in_specs, out_specs=out_specs, check_vma=False
    )
```

```python
import functools

import jax
import jax.numpy as jnp
from jax import lax
from jax.experimental import pallas as pl
from jax.experimental.pallas import tpu as pltpu
from jax.sharding import PartitionSpec as P

TLEN = 150
WINDOW = 450
EPS = 1e-06
CAP = 8
ROWS_DEV = 16
STATIONS = 32
LAGS = 512
WIDE = 768
DEPTH = 512
SLOTS = 128
CHUNKS = 8
SPAN = STATIONS // CHUNKS
AHEAD = 3
CHIPS = 8
BLOCKS = 16
REGIONS = 16
FAR = 4
PIECES = 4
PIECE = 256 // PIECES
MESH = pl.DeviceIdType.MESH


def kernel(
    waves_ref, own_ref, number_ref, out_ref,
    bank, hankel, shifts, wave, halo_out, halo_in, scale_ref, corr, rows_ref, total,
    outgo, income, part, gathered,
    halo_sem, ring_send, ring_recv, share_send, share_recv, side_send, side_recv,
    spread_send, spread_recv,
):
    block = lax.axis_index("tmpl")
    region = lax.axis_index("sta")
    z = block // 2
    core = block % 2
    other = 1 - core

    def at(chip, which):
        return (lax.rem(chip + CHIPS, CHIPS) * 2 + which, region)

    barrier = pltpu.get_barrier_semaphore()
    near = [at(z, other), at(z + 1, core), at(z - 1, core), at(z + 2 * core - 1, other)]
    near += [(block, lax.rem(region + side, REGIONS)) for side in (1, REGIONS - 1)]
    for device in near:
        pl.semaphore_signal(barrier, inc=1, device_id=device, device_id_type=MESH)

    coarse = waves_ref[...].astype(jnp.bfloat16)
    halo_out[...] = coarse[:, :256]
    for tile in range(4):
        wave[tile] = coarse[:, tile * 128 : tile * 128 + 128].astype(jnp.float32)

    slot = lax.broadcasted_iota(jnp.int32, (STATIONS * CAP, CAP), 0) & 7
    expand = slot == lax.broadcasted_iota(jnp.int32, (STATIONS * CAP, CAP), 1)
    expand = expand.astype(jnp.bfloat16)
    mine = lax.broadcasted_iota(jnp.int32, (STATIONS * CAP, STATIONS), 0) >> 3
    mine = mine == lax.broadcasted_iota(jnp.int32, (STATIONS * CAP, STATIONS), 1)
    lane = lax.broadcasted_iota(jnp.int32, (STATIONS * CAP, 128), 1)
    numbers = jnp.zeros((STATIONS * CAP, 128), jnp.float32)
    for i, digits in enumerate((number_ref[...] >> 6, number_ref[...] & 63)):
        digits = digits.astype(jnp.float32).astype(jnp.bfloat16)
        column = jnp.dot(expand, digits, preferred_element_type=jnp.float32)
        column = jnp.sum(jnp.where(mine, column, 0.0), axis=1, keepdims=True)
        numbers = jnp.where(lane == WINDOW - 384 + i, column, numbers)
    bank[block, :, :384] = own_ref[:, :384]
    bank[block, :, 384:] = numbers.astype(jnp.bfloat16)
    bank[block, :, 384:WINDOW] = own_ref[:, 384:]
    pl.semaphore_wait(barrier, len(near))

    to_left = pltpu.make_async_remote_copy(
        src_ref=halo_out,
        dst_ref=halo_in,
        send_sem=halo_sem.at[0],
        recv_sem=halo_sem.at[1],
        device_id=(lax.rem(block + BLOCKS - 1, BLOCKS), region),
        device_id_type=MESH,
    )
    to_left.start()

    def place(chunk, chip, which):
        first = pl.multiple_of(chunk * SPAN * CAP, SPAN * CAP)
        return bank.at[lax.rem(chip + CHIPS, CHIPS) * 2 + which, pl.ds(first, SPAN * CAP), :]

    def ring(way, chunk, hop, origin):
        ref = place(chunk, origin, core)
        return pltpu.make_async_remote_copy(
            src_ref=ref,
            dst_ref=ref,
            send_sem=ring_send,
            recv_sem=ring_recv.at[way, chunk, hop],
            device_id=at(z + (1 if way == 0 else -1), core),
            device_id_type=MESH,
        )

    def share(chunk, chip):
        ref = place(chunk, chip, core)
        return pltpu.make_async_remote_copy(
            src_ref=ref,
            dst_ref=ref,
            send_sem=share_send,
            recv_sem=share_recv.at[chunk],
            device_id=at(z, other),
            device_id_type=MESH,
        )

    def bulk(count, send, receive):
        ref = bank.at[pl.ds(0, count // CHUNKS)]
        return pltpu.make_async_remote_copy(
            src_ref=ref, dst_ref=ref, send_sem=send, recv_sem=receive,
            device_id=at(z, other), device_id_type=MESH,
        )

    def inject(chunk):
        for way in range(2):
            ring(way, chunk, 0, z).start()
        share(chunk, z).start()

    for chunk in range(AHEAD + 1):
        inject(chunk)

    total[...] = jnp.zeros_like(total)

    def waves_ready():
        to_left.wait()
        last = jnp.where(block == BLOCKS - 1, 0.0, 1.0)
        for tile in range(2):
            one = halo_in[:, tile * 128 : tile * 128 + 128]
            wave[4 + tile] = one.astype(jnp.float32) * last
        every = jnp.concatenate([wave[tile] for tile in range(6)], axis=1)
        for lane in range(16):
            moved = every if lane == 0 else pltpu.roll(every, WIDE - lane, 1)
            for tile in range(6):
                shifts[tile, pl.ds(lane, 96, stride=16), :] = moved[:, tile * 128 : tile * 128 + 128]
        pieces = []
        for tile in range(6):
            squared = jnp.zeros((STATIONS, 128), jnp.float32)
            for channel in range(3):
                one = wave[tile, pl.ds(channel * STATIONS, STATIONS), :]
                squared = squared + one * one
            pieces.append(squared)
        squared = jnp.concatenate(pieces, axis=1)
        def left(x, by):
            return pltpu.roll(x, WIDE - by, 1)
        two = squared + left(squared, 1)
        four = two + left(two, 2)
        run = four
        for by in (4, 8):
            run = run + left(run, by)
        sixteen = run
        for by in (16, 32, 64):
            run = run + left(run, by)
        run = run + left(sixteen, 128) + left(four, 144) + left(two, 148)
        scale_ref[...] = lax.rsqrt(run[:, :LAGS] / WINDOW + EPS)

    lower = lax.broadcasted_iota(jnp.int32, (16, LAGS), 0)

    def build(station):
        rolled = []
        for c in range(3):
            rows = pl.ds(pl.multiple_of((c * STATIONS + station) * 16, 16), 16)
            rolled.append(jnp.concatenate([shifts[tile, rows, :] for tile in range(6)], axis=1))

        def taken(channel, start):
            if start == 0:
                return rolled[channel][:, :LAGS]
            return pltpu.roll(rolled[channel], (WIDE - start) % WIDE, 1)[:, :LAGS]

        for tile in range(DEPTH // 16):
            first = tile * 16
            if first >= WINDOW:
                value = jnp.zeros((16, LAGS), jnp.float32)
            else:
                channel, start = divmod(first, TLEN)
                value = taken(channel, start)
                rest = TLEN - start
                if rest < 16:
                    if channel < 2:
                        after = taken(channel + 1, start - TLEN)
                    else:
                        after = jnp.zeros((16, LAGS), jnp.float32)
                    value = jnp.where(lower < rest, value, after)
            hankel[station, pl.ds(first, 16), :] = value.astype(jnp.bfloat16)

    ids = lax.broadcasted_iota(jnp.int32, (16, SLOTS), 1)
    picker = jnp.where(ids == WINDOW - 384, 64.0, jnp.where(ids == WINDOW + 1 - 384, 1.0, 0.0))
    picker = picker.astype(jnp.bfloat16)
    live = lax.broadcasted_iota(jnp.int32, (SLOTS, 128), 1) < WINDOW - 384

    def correlate(pair, where):
        rows = pl.ds(pl.multiple_of(pair * 16, 16), 16)
        both = [bank[b, rows, :].astype(jnp.float32) for b in range(BLOCKS)]
        for i in range(2):
            one(pair * 2 + i, where * 2 + i, [x[i * 8 : i * 8 + 8] for x in both])

    def one(station, where, pieces):
        wide = jnp.concatenate(pieces, axis=0)
        waves = wide.astype(jnp.bfloat16)
        product = jnp.dot(waves, hankel[station], preferred_element_type=jnp.float32)
        last = jnp.where(live, wide[:, 384:], 0.0)
        power = last * last
        for tile in range(3):
            power = power + wide[:, tile * 128 : tile * 128 + 128] * wide[:, tile * 128 : tile * 128 + 128]
        power = jnp.sum(power, axis=1, keepdims=True)
        factor = lax.rsqrt(power / WINDOW + EPS) / WINDOW
        value = product * factor * scale_ref[pl.ds(station, 1), :]
        start = pl.multiple_of(where * SLOTS, SLOTS)
        corr[pl.ds(start, SLOTS), :] = value.astype(jnp.bfloat16)
        row = lax.dot_general(
            picker, waves[:, 384:], (((1,), (1,)), ((), ())), preferred_element_type=jnp.float32
        )
        row = row[:8].astype(jnp.int32)
        group = row >> 8
        home = (row >> 4) & 15
        relative = (home - region + 1 + REGIONS) & 15
        apart = ((group >> 1) - z + CHIPS) & 7
        order = jnp.where(apart >= 4, 2 * apart - 8, 7 - 2 * apart)
        index = relative * 256 + (order * 2 + (group & 1)) * ROWS_DEV + (row & 15)
        index = jnp.where(row < 4096, index, 4096)
        rows_ref[where] = index

    across = lax.broadcasted_iota(jnp.int32, (256, SLOTS), 0).astype(jnp.float32).astype(jnp.bfloat16)

    def scatter(relative):
        picks = []
        for i in range(SPAN):
            index = rows_ref[i] - relative * 256
            index = jnp.where((index >= 0) & (index < 256), index, 512)
            index = index.astype(jnp.float32).astype(jnp.bfloat16)
            same = across == jnp.broadcast_to(index[:1], (256, SLOTS))
            picks.append(jnp.where(same, jnp.bfloat16(1), jnp.bfloat16(0)))
        selector = jnp.concatenate(picks, axis=1)
        start = relative * 256
        total[pl.ds(start, 256), :] += jnp.dot(
            selector, corr[...], preferred_element_type=jnp.float32
        )

    def moves(turn):
        for hop in range(FAR):
            chunk = turn - 1 - hop
            inside = (chunk >= 0) & (chunk < CHUNKS)
            for way in range(2):
                sign = -1 if way == 0 else 1
                arrives = inside
                if hop == FAR - 1:
                    arrives = inside & (lax.rem(chunk + CHUNKS, 2) == way)

                @pl.when(arrives)
                def _():
                    origin = z + sign * (hop + 1)
                    ring(way, chunk, hop, origin).wait_recv()
                    if hop + 1 < FAR - 1:
                        ring(way, chunk, hop + 1, origin).start()
                    elif hop + 1 == FAR - 1:

                        @pl.when(lax.rem(chunk, 2) == way)
                        def _():
                            ring(way, chunk, hop + 1, origin).start()

                    share(chunk, origin).start()

        @pl.when((turn >= 1) & (turn + AHEAD < CHUNKS))
        def _():
            inject(turn + AHEAD)

    def spots(chunk):
        for i in range(SPAN // 2):
            correlate(chunk * (SPAN // 2) + i, i)

    @pl.loop(0, CHUNKS + FAR)
    def _(turn):
        moves(turn)

        @pl.when(turn == 0)
        def _():
            waves_ready()

        @pl.when(turn < CHUNKS)
        def _():
            @pl.loop(0, SPAN)
            def _(i):
                build(turn * SPAN + i)

        @pl.when(turn > FAR)
        def _():
            for relative in range(3):
                scatter(relative)

        @pl.when(turn >= FAR)
        def _():
            chunk = turn - FAR
            bulk(CHUNKS, share_send, share_recv.at[chunk]).wait_recv()
            spots(chunk)

    def side(direction, piece):
        step = REGIONS - 1 if direction == 0 else 1
        span = pl.ds(piece * PIECE, PIECE)
        return pltpu.make_async_remote_copy(
            src_ref=outgo.at[direction, span],
            dst_ref=income.at[direction, span],
            send_sem=side_send.at[direction, piece],
            recv_sem=side_recv.at[direction, piece],
            device_id=(block, lax.rem(region + step, REGIONS)),
            device_id_type=MESH,
        )

    for direction in range(2):
        scatter(2 * direction)
        outgo[direction] = total[pl.ds(512 * direction, 256), :].astype(jnp.bfloat16)
        for piece in range(PIECES):
            side(direction, piece).start()
    scatter(1)

    def spread(piece, slot):
        order = piece * 2 + slot // 2
        apart = 4 + order // 2 if order % 2 == 0 else 3 - order // 2
        return order, apart, slot % 2

    def send_out(order, apart, which):
        rows = pl.ds((order * 2 + which) * ROWS_DEV, ROWS_DEV)
        return pltpu.make_async_remote_copy(
            src_ref=part.at[rows],
            dst_ref=gathered.at[block],
            send_sem=spread_send.at[order * 2 + which],
            recv_sem=spread_recv.at[block],
            device_id=at(z + apart, which),
            device_id_type=MESH,
        )

    for piece in range(PIECES):
        for direction in range(2):
            side(direction, piece).wait_recv()
        span = pl.ds(piece * PIECE, PIECE)
        summed = total[pl.ds(256 + piece * PIECE, PIECE), :]
        summed = summed + income[0, span].astype(jnp.float32) + income[1, span].astype(jnp.float32)
        part[span] = summed.astype(jnp.bfloat16)
        for slot in range(4):
            order, apart, which = spread(piece, slot)
            if apart == 0:

                @pl.when(core != which)
                def _():
                    send_out(order, apart, which).start()

            else:
                send_out(order, apart, which).start()

    here = pl.ds(pl.multiple_of((14 + core) * ROWS_DEV, ROWS_DEV), ROWS_DEV)
    gathered[block] = part[here]

    bulk(CHUNKS * 7, ring_send, share_recv.at[0]).wait_send()
    bulk(CHUNKS * 8, share_send, share_recv.at[0]).wait_send()
    for direction in range(2):
        for piece in range(PIECES):
            side(direction, piece).wait_send()

    def spread_wait(source):
        return pltpu.make_async_remote_copy(
            src_ref=part.at[pl.ds(0, ROWS_DEV)],
            dst_ref=gathered.at[source],
            send_sem=spread_send.at[0],
            recv_sem=spread_recv.at[source],
            device_id=(block, region),
            device_id_type=MESH,
        )

    for piece in range(PIECES):
        for slot in range(4):
            order, apart, which = spread(piece, slot)
            if apart == 0:

                @pl.when(core != which)
                def _():
                    send_out(order, apart, which).wait_send()

            else:
                send_out(order, apart, which).wait_send()

    @pl.loop(1, BLOCKS)
    def _(step):
        spread_wait(lax.rem(block + step, BLOCKS)).wait_recv()

    for source in range(BLOCKS):
        out_ref[:, pl.ds(source * LAGS, LAGS)] = gathered[source]


def on_device(waveforms, templates, pair_rows):
    waves = waveforms.transpose(1, 0, 2).reshape(STATIONS * 3, LAGS)
    own = templates.reshape(STATIONS * CAP, WINDOW)
    bf16, f32 = jnp.bfloat16, jnp.float32
    dma = pltpu.SemaphoreType.DMA
    result = pl.pallas_call(
        kernel,
        out_shape=jax.ShapeDtypeStruct((ROWS_DEV, BLOCKS * LAGS), bf16),
        in_specs=[pl.BlockSpec(memory_space=pltpu.VMEM)] * 3,
        out_specs=pl.BlockSpec(memory_space=pltpu.VMEM),
        scratch_shapes=[
            pltpu.VMEM((BLOCKS, STATIONS * CAP, DEPTH), bf16),
            pltpu.VMEM((STATIONS, DEPTH, LAGS), bf16),
            pltpu.VMEM((6, STATIONS * 3 * 16, 128), f32),
            pltpu.VMEM((6, STATIONS * 3, 128), f32),
            pltpu.VMEM((STATIONS * 3, 256), bf16),
            pltpu.VMEM((STATIONS * 3, 256), bf16),
            pltpu.VMEM((STATIONS, LAGS), f32),
            pltpu.VMEM((SPAN * SLOTS, LAGS), bf16),
            pltpu.VMEM((SPAN, 8, SLOTS), jnp.int32),
            pltpu.VMEM((768, LAGS), f32),
            pltpu.VMEM((2, 256, LAGS), bf16),
            pltpu.VMEM((2, 256, LAGS), bf16),
            pltpu.VMEM((256, LAGS), bf16),
            pltpu.VMEM((BLOCKS, ROWS_DEV, LAGS), bf16),
            dma((2,)),
            dma,
            dma((2, CHUNKS, FAR)),
            dma,
            dma((CHUNKS,)),
            dma((2, PIECES)),
            dma((2, PIECES)),
            dma((BLOCKS,)),
            dma((BLOCKS,)),
        ],
        compiler_params=pltpu.CompilerParams(
            collective_id=0, has_side_effects=True, vmem_limit_bytes=60 * 1024 * 1024
        ),
    )(waves, own, pair_rows.T)
    return result.astype(jnp.float32)


def solution(mesh):
    in_specs = (P("sta", None, "tmpl"), P("sta", "tmpl", None), P("sta", "tmpl"))
    out_specs = P(("tmpl", "sta"), None)
    return jax.shard_map(
        on_device, mesh=mesh, in_specs=in_specs, out_specs=out_specs, check_vma=False
    )
```

```python
import functools

import jax
import jax.numpy as jnp
from jax import lax
from jax.experimental import pallas as pl
from jax.experimental.pallas import tpu as pltpu
from jax.sharding import PartitionSpec as P

TLEN = 150
WINDOW = 450
EPS = 1e-06
CAP = 8
ROWS_DEV = 16
STATIONS = 32
LAGS = 512
WIDE = 768
DEPTH = 512
SLOTS = 128
CHUNKS = 8
SPAN = STATIONS // CHUNKS
AHEAD = 3
CHIPS = 8
BLOCKS = 16
REGIONS = 16
FAR = 4
WHEN = (1, 4, 7, 10)
READY = WHEN[-1] + 1
TICKS = READY + 2 * (CHUNKS - 1)
PIECES = 4
PIECE = 256 // PIECES
MESH = pl.DeviceIdType.MESH


def kernel(
    waves_ref, own_ref, number_ref, out_ref,
    bank, extra, last_tile, hankel, shifts, wave, halo_out, halo_in, scale_ref, corr, rows_ref, total,
    outgo, income, part, gathered,
    halo_sem, ring_send, ring_recv, share_send, share_recv, extra_send, extra_recv, extra_share,
    side_send, side_recv, spread_send, spread_recv,
):
    block = lax.axis_index("tmpl")
    region = lax.axis_index("sta")
    z = block // 2
    core = block % 2
    other = 1 - core

    def at(chip, which):
        return (lax.rem(chip + CHIPS, CHIPS) * 2 + which, region)

    barrier = pltpu.get_barrier_semaphore()
    near = [at(z, other), at(z + 1, core), at(z - 1, core), at(z + 2 * core - 1, other)]
    near += [(block, lax.rem(region + side, REGIONS)) for side in (1, REGIONS - 1)]
    for device in near:
        pl.semaphore_signal(barrier, inc=1, device_id=device, device_id_type=MESH)

    lane8 = lax.broadcasted_iota(jnp.int32, (CAP, 128), 1)
    coarse = waves_ref[...].astype(jnp.bfloat16)
    halo_out[...] = coarse[:, :256]
    for tile in range(4):
        wave[tile] = coarse[:, tile * 128 : tile * 128 + 128].astype(jnp.float32)

    last_tile[...] = jnp.zeros_like(last_tile)
    last_tile[:, : WINDOW - 384] = own_ref[:, 384:].astype(jnp.float32)
    for chunk in range(CHUNKS):
        rows = pl.ds(chunk * SPAN * CAP, SPAN * CAP)
        for tile in range(3):
            bank[block, chunk, pl.ds(tile * SPAN * CAP, SPAN * CAP), :] = own_ref[
                rows, tile * 128 : tile * 128 + 128
            ]
        ends = [last_tile[pl.ds((chunk * SPAN + i) * CAP, CAP), :] for i in range(SPAN)]
        joined = [
            jnp.where(lane8 < 64, ends[i], pltpu.roll(ends[i + 1], 64, 1)) for i in range(0, SPAN, 2)
        ]
        bank[block, chunk, pl.ds(3 * SPAN * CAP, SPAN * CAP // 2), :] = jnp.concatenate(
            joined, axis=0
        ).astype(jnp.bfloat16)
    spread_lane = lax.broadcasted_iota(jnp.int32, (STATIONS, 128), 1)
    spread_row = lax.broadcasted_iota(jnp.int32, (STATIONS, 128), 0)
    extras = jnp.zeros((CAP, 128), jnp.float32)
    for i, digits in enumerate((number_ref[...] >> 6, number_ref[...] & 63)):
        digits = digits.astype(jnp.float32).astype(jnp.bfloat16)
        selects = (spread_lane == spread_row * 4 + 2 + i).astype(jnp.bfloat16)
        extras = extras + jnp.dot(digits, selects, preferred_element_type=jnp.float32)
    for station in range(STATIONS):
        moved = pltpu.roll(last_tile[pl.ds(station * CAP, CAP), :], (station * 4 + 64) % 128, 1)
        extras = jnp.where((lane8 >> 1) == station * 2, moved, extras)
    extra[block] = jnp.concatenate([extras, jnp.zeros_like(extras)], axis=0).astype(jnp.bfloat16)
    pl.semaphore_wait(barrier, len(near))

    to_left = pltpu.make_async_remote_copy(
        src_ref=halo_out,
        dst_ref=halo_in,
        send_sem=halo_sem.at[0],
        recv_sem=halo_sem.at[1],
        device_id=(lax.rem(block + BLOCKS - 1, BLOCKS), region),
        device_id_type=MESH,
    )
    to_left.start()

    def index_of(chip):
        return lax.rem(chip + CHIPS, CHIPS) * 2 + core

    def remote(ref, send, receive, device):
        return pltpu.make_async_remote_copy(
            src_ref=ref, dst_ref=ref, send_sem=send, recv_sem=receive,
            device_id=device, device_id_type=MESH,
        )

    ahead = [at(z + 1, core), at(z - 1, core)]
    mate = at(z, other)

    def ring(way, chunk, hop, origin):
        ref = bank.at[index_of(origin), chunk]
        remote(ref, ring_send, ring_recv.at[chunk, hop], ahead[way]).start()

    def share(chunk, chip):
        remote(bank.at[index_of(chip), chunk], share_send, share_recv.at[chunk], mate).start()

    def ring_extra(way, hop, origin):
        remote(extra.at[index_of(origin)], extra_send, extra_recv.at[hop], ahead[way]).start()

    def share_extra(chip):
        remote(extra.at[index_of(chip)], extra_send, extra_share, mate).start()

    def inject(chunk):
        for way in range(2):
            ring(way, chunk, 0, z)
        share(chunk, z)

    for way in range(2):
        ring_extra(way, 0, z)
    for chunk in range(AHEAD + 1):
        inject(chunk)
    share_extra(z)

    total[...] = jnp.zeros_like(total)

    def waves_ready():
        to_left.wait()
        last = jnp.where(block == BLOCKS - 1, 0.0, 1.0)
        for tile in range(2):
            one = halo_in[:, tile * 128 : tile * 128 + 128]
            wave[4 + tile] = one.astype(jnp.float32) * last
        every = jnp.concatenate([wave[tile] for tile in range(6)], axis=1)
        for lane in range(16):
            moved = every if lane == 0 else pltpu.roll(every, WIDE - lane, 1)
            for tile in range(6):
                shifts[tile, pl.ds(lane, 96, stride=16), :] = moved[:, tile * 128 : tile * 128 + 128]
        pieces = []
        for tile in range(6):
            squared = jnp.zeros((STATIONS, 128), jnp.float32)
            for channel in range(3):
                one = wave[tile, pl.ds(channel * STATIONS, STATIONS), :]
                squared = squared + one * one
            pieces.append(squared)
        squared = jnp.concatenate(pieces, axis=1)
        def left(x, by):
            return pltpu.roll(x, WIDE - by, 1)
        two = squared + left(squared, 1)
        four = two + left(two, 2)
        run = four
        for by in (4, 8):
            run = run + left(run, by)
        sixteen = run
        for by in (16, 32, 64):
            run = run + left(run, by)
        run = run + left(sixteen, 128) + left(four, 144) + left(two, 148)
        scale_ref[...] = lax.rsqrt(run[:, :LAGS] / WINDOW + EPS)

    lower = lax.broadcasted_iota(jnp.int32, (16, LAGS), 0)

    def build(station):
        rolled = []
        for c in range(3):
            rows = pl.ds(pl.multiple_of((c * STATIONS + station) * 16, 16), 16)
            rolled.append(jnp.concatenate([shifts[tile, rows, :] for tile in range(6)], axis=1))

        def taken(channel, start):
            if start == 0:
                return rolled[channel][:, :LAGS]
            return pltpu.roll(rolled[channel], (WIDE - start) % WIDE, 1)[:, :LAGS]

        for tile in range(DEPTH // 16):
            first = tile * 16
            if first >= WINDOW:
                value = jnp.zeros((16, LAGS), jnp.float32)
            else:
                channel, start = divmod(first, TLEN)
                value = taken(channel, start)
                rest = TLEN - start
                if rest < 16:
                    if channel < 2:
                        after = taken(channel + 1, start - TLEN)
                    else:
                        after = jnp.zeros((16, LAGS), jnp.float32)
                    value = jnp.where(lower < rest, value, after)
            hankel[station, pl.ds(first, 16), :] = value.astype(jnp.bfloat16)

    ids = lax.broadcasted_iota(jnp.int32, (16, SLOTS), 1)
    picker = jnp.where(ids == WINDOW - 384, 64.0, jnp.where(ids == WINDOW + 1 - 384, 1.0, 0.0))
    picker = picker.astype(jnp.bfloat16)
    live = lax.broadcasted_iota(jnp.int32, (SLOTS, 128), 1) < WINDOW - 384

    lane_all = lax.broadcasted_iota(jnp.int32, (SLOTS, 128), 1)

    def correlate(chunk, pair, slot):
        tiles = []
        for tile in range(3):
            rows = pl.ds(pl.multiple_of(tile * SPAN * CAP + pair * 16, 16), 16)
            tiles.append([bank[b, chunk, rows, :].astype(jnp.float32) for b in range(BLOCKS)])
        rows = pl.ds(3 * SPAN * CAP, 16)
        ends = [bank[b, chunk, rows, :].astype(jnp.float32) for b in range(BLOCKS)]
        ends = jnp.concatenate([jnp.where(pair == 0, x[:8], x[8:]) for x in ends], axis=0)
        extras = jnp.concatenate([extra[b].astype(jnp.float32)[:8] for b in range(BLOCKS)], axis=0)
        for i in range(2):
            station = chunk * SPAN + pair * 2 + i
            end = ends if i == 0 else pltpu.roll(ends, 64, 1)
            few = pltpu.roll(extras, lax.rem(192 - station * 4, 128), 1)
            end = jnp.where(lane_all < 64, end, jnp.where(lane_all < 68, few, 0.0))
            pieces = [jnp.concatenate([x[i * 8 : i * 8 + 8] for x in t], axis=0) for t in tiles]
            one(station, slot, pair * 2 + i, jnp.concatenate(pieces + [end], axis=1))

    def one(station, slot, where, wide):
        waves = wide.astype(jnp.bfloat16)
        product = jnp.dot(waves, hankel[station], preferred_element_type=jnp.float32)
        last = jnp.where(live, wide[:, 384:], 0.0)
        power = last * last
        for tile in range(3):
            power = power + wide[:, tile * 128 : tile * 128 + 128] * wide[:, tile * 128 : tile * 128 + 128]
        power = jnp.sum(power, axis=1, keepdims=True)
        factor = lax.rsqrt(power / WINDOW + EPS) / WINDOW
        value = product * factor * scale_ref[pl.ds(station, 1), :]
        start = pl.multiple_of(where * SLOTS, SLOTS)
        corr[slot, pl.ds(start, SLOTS), :] = value.astype(jnp.bfloat16)
        row = lax.dot_general(
            picker, waves[:, 384:], (((1,), (1,)), ((), ())), preferred_element_type=jnp.float32
        )
        row = row[:8].astype(jnp.int32)
        group = row >> 8
        home = (row >> 4) & 15
        relative = (home - region + 1 + REGIONS) & 15
        apart = ((group >> 1) - z + CHIPS) & 7
        order = jnp.where(apart >= 4, 2 * apart - 8, 7 - 2 * apart)
        index = relative * 256 + (order * 2 + (group & 1)) * ROWS_DEV + (row & 15)
        index = jnp.where(row < 4096, index, 4096)
        rows_ref[slot, where] = index

    across = lax.broadcasted_iota(jnp.int32, (256, SLOTS), 0).astype(jnp.float32).astype(jnp.bfloat16)

    def scatter(relative, slot):
        picks = []
        for i in range(SPAN):
            index = rows_ref[slot, i] - relative * 256
            index = jnp.where((index >= 0) & (index < 256), index, 512)
            index = index.astype(jnp.float32).astype(jnp.bfloat16)
            same = across == jnp.broadcast_to(index[:1], (256, SLOTS))
            picks.append(jnp.where(same, jnp.bfloat16(1), jnp.bfloat16(0)))
        selector = jnp.concatenate(picks, axis=1)
        start = relative * 256
        total[pl.ds(start, 256), :] += jnp.dot(
            selector, corr[slot], preferred_element_type=jnp.float32
        )

    def pair_of(ref, count):
        return ref.at[0, pl.ds(0, count)]

    def moves(tick):
        for hop in range(FAR):
            late = tick - WHEN[hop]

            @pl.when((late >= 0) & (late < 2 * CHUNKS) & (lax.rem(late + 2 * TICKS, 2) == 0))
            def _():
                chunk = lax.div(late, 2)
                count = 2 if hop < FAR - 1 else 1
                arrived = bank.at[0, pl.ds(0, count)]
                remote(arrived, ring_send, ring_recv.at[chunk, hop], mate).wait_recv()
                for way in range(2):
                    origin = z + (-1 if way == 0 else 1) * (hop + 1)
                    if hop + 1 < FAR - 1:
                        ring(way, chunk, hop + 1, origin)
                        share(chunk, origin)
                    elif hop + 1 == FAR - 1:

                        @pl.when(lax.rem(chunk, 2) == way)
                        def _():
                            ring(way, chunk, hop + 1, origin)

                        share(chunk, origin)
                if hop == FAR - 1:
                    share(chunk, z + FAR)

            if hop < FAR - 1:

                @pl.when(tick == WHEN[hop])
                def _():
                    remote(extra.at[pl.ds(0, 2)], extra_send, extra_recv.at[hop], mate).wait_recv()
                    for way in range(2):
                        origin = z + (-1 if way == 0 else 1) * (hop + 1)
                        if hop + 1 < FAR - 1 or way == 0:
                            ring_extra(way, hop + 1, origin)
                        share_extra(origin)

            else:

                @pl.when(tick == WHEN[hop])
                def _():
                    remote(extra.at[0], extra_send, extra_recv.at[hop], mate).wait_recv()
                    share_extra(z + FAR)

        @pl.when((tick > 0) & (lax.rem(tick, 2) == 0) & (lax.div(tick, 2) + AHEAD < CHUNKS))
        def _():
            inject(lax.div(tick, 2) + AHEAD)

    def shared(chunk):
        remote(bank.at[pl.ds(0, CHIPS), 0], share_send, share_recv.at[chunk], mate).wait_recv()

    waves_ready()

    @pl.loop(0, TICKS)
    def _(tick):
        moves(tick)

        @pl.when(tick < CHUNKS)
        def _():
            @pl.loop(0, SPAN)
            def _(i):
                build(tick * SPAN + i)

        @pl.when(tick == READY)
        def _():
            remote(extra.at[pl.ds(0, CHIPS)], extra_send, extra_share, mate).wait_recv()

        @pl.when(tick >= READY)
        def _():
            step = tick - READY
            chunk = lax.div(step, 2)
            pair = lax.rem(step, 2)

            @pl.when((step >= 2) & (pair == 0))
            def _():
                slot = lax.rem(chunk + 1, 2)
                scatter(0, slot)
                scatter(1, slot)

            @pl.when((step >= 2) & (pair == 1))
            def _():
                scatter(2, lax.rem(chunk + 1, 2))

            @pl.when(pair == 0)
            def _():
                shared(chunk)

            correlate(chunk, pair, lax.rem(chunk, 2))

    for relative in range(3):
        scatter(relative, CHUNKS % 2)
    shared(CHUNKS - 1)

    @pl.loop(0, 2)
    def _(pair):
        correlate(CHUNKS - 1, pair, 1 - CHUNKS % 2)

    def side(direction, piece):
        step = REGIONS - 1 if direction == 0 else 1
        span = pl.ds(piece * PIECE, PIECE)
        return pltpu.make_async_remote_copy(
            src_ref=outgo.at[direction, span],
            dst_ref=income.at[direction, span],
            send_sem=side_send.at[direction, piece],
            recv_sem=side_recv.at[direction, piece],
            device_id=(block, lax.rem(region + step, REGIONS)),
            device_id_type=MESH,
        )

    for direction in range(2):
        scatter(2 * direction, 1 - CHUNKS % 2)
        outgo[direction] = total[pl.ds(512 * direction, 256), :].astype(jnp.bfloat16)
        for piece in range(PIECES):
            side(direction, piece).start()
    scatter(1, 1 - CHUNKS % 2)

    def spread(piece, slot):
        order = piece * 2 + slot // 2
        apart = 4 + order // 2 if order % 2 == 0 else 3 - order // 2
        return order, apart, slot % 2

    def send_out(order, apart, which):
        rows = pl.ds((order * 2 + which) * ROWS_DEV, ROWS_DEV)
        return pltpu.make_async_remote_copy(
            src_ref=part.at[rows],
            dst_ref=gathered.at[block],
            send_sem=spread_send.at[order * 2 + which],
            recv_sem=spread_recv.at[block],
            device_id=at(z + apart, which),
            device_id_type=MESH,
        )

    for piece in range(PIECES):
        for direction in range(2):
            side(direction, piece).wait_recv()
        span = pl.ds(piece * PIECE, PIECE)
        summed = total[pl.ds(256 + piece * PIECE, PIECE), :]
        summed = summed + income[0, span].astype(jnp.float32) + income[1, span].astype(jnp.float32)
        part[span] = summed.astype(jnp.bfloat16)
        for slot in range(4):
            order, apart, which = spread(piece, slot)
            if apart == 0:

                @pl.when(core != which)
                def _():
                    send_out(order, apart, which).start()

            else:
                send_out(order, apart, which).start()

    here = pl.ds(pl.multiple_of((14 + core) * ROWS_DEV, ROWS_DEV), ROWS_DEV)
    gathered[block] = part[here]

    remote(bank.at[pl.ds(0, 7)], ring_send, share_recv.at[0], mate).wait_send()
    remote(bank.at[pl.ds(0, 8)], share_send, share_recv.at[0], mate).wait_send()
    remote(extra.at[pl.ds(0, 15)], extra_send, extra_share, mate).wait_send()
    for direction in range(2):
        for piece in range(PIECES):
            side(direction, piece).wait_send()

    def spread_wait(source):
        return pltpu.make_async_remote_copy(
            src_ref=part.at[pl.ds(0, ROWS_DEV)],
            dst_ref=gathered.at[source],
            send_sem=spread_send.at[0],
            recv_sem=spread_recv.at[source],
            device_id=(block, region),
            device_id_type=MESH,
        )

    for piece in range(PIECES):
        for slot in range(4):
            order, apart, which = spread(piece, slot)
            if apart == 0:

                @pl.when(core != which)
                def _():
                    send_out(order, apart, which).wait_send()

            else:
                send_out(order, apart, which).wait_send()

    @pl.loop(1, BLOCKS)
    def _(step):
        spread_wait(lax.rem(block + step, BLOCKS)).wait_recv()

    for source in range(BLOCKS):
        out_ref[:, pl.ds(source * LAGS, LAGS)] = gathered[source]


def on_device(waveforms, templates, pair_rows):
    waves = waveforms.transpose(1, 0, 2).reshape(STATIONS * 3, LAGS)
    own = templates.reshape(STATIONS * CAP, WINDOW)
    bf16, f32 = jnp.bfloat16, jnp.float32
    dma = pltpu.SemaphoreType.DMA
    result = pl.pallas_call(
        kernel,
        out_shape=jax.ShapeDtypeStruct((ROWS_DEV, BLOCKS * LAGS), bf16),
        in_specs=[pl.BlockSpec(memory_space=pltpu.VMEM)] * 3,
        out_specs=pl.BlockSpec(memory_space=pltpu.VMEM),
        scratch_shapes=[
            pltpu.VMEM((BLOCKS, CHUNKS, 7 * SPAN * CAP // 2, 128), bf16),
            pltpu.VMEM((BLOCKS, 16, 128), bf16),
            pltpu.VMEM((STATIONS * CAP, 128), f32),
            pltpu.VMEM((STATIONS, DEPTH, LAGS), bf16),
            pltpu.VMEM((6, STATIONS * 3 * 16, 128), f32),
            pltpu.VMEM((6, STATIONS * 3, 128), f32),
            pltpu.VMEM((STATIONS * 3, 256), bf16),
            pltpu.VMEM((STATIONS * 3, 256), bf16),
            pltpu.VMEM((STATIONS, LAGS), f32),
            pltpu.VMEM((2, SPAN * SLOTS, LAGS), bf16),
            pltpu.VMEM((2, SPAN, 8, SLOTS), jnp.int32),
            pltpu.VMEM((768, LAGS), f32),
            pltpu.VMEM((2, 256, LAGS), bf16),
            pltpu.VMEM((2, 256, LAGS), bf16),
            pltpu.VMEM((256, LAGS), bf16),
            pltpu.VMEM((BLOCKS, ROWS_DEV, LAGS), bf16),
            dma((2,)),
            dma,
            dma((CHUNKS, FAR)),
            dma,
            dma((CHUNKS,)),
            dma,
            dma((FAR,)),
            dma,
            dma((2, PIECES)),
            dma((2, PIECES)),
            dma((BLOCKS,)),
            dma((BLOCKS,)),
        ],
        compiler_params=pltpu.CompilerParams(
            collective_id=0, has_side_effects=True, vmem_limit_bytes=60 * 1024 * 1024
        ),
    )(waves, own, pair_rows.T)
    return result.astype(jnp.float32)


def solution(mesh):
    in_specs = (P("sta", None, "tmpl"), P("sta", "tmpl", None), P("sta", "tmpl"))
    out_specs = P(("tmpl", "sta"), None)
    return jax.shard_map(
        on_device, mesh=mesh, in_specs=in_specs, out_specs=out_specs, check_vma=False
    )
```

```python
import functools

import jax
import jax.numpy as jnp
from jax import lax
from jax.experimental import pallas as pl
from jax.experimental.pallas import tpu as pltpu
from jax.sharding import PartitionSpec as P

TLEN = 150
WINDOW = 450
EPS = 1e-06
CAP = 8
ROWS_DEV = 16
STATIONS = 32
LAGS = 512
WIDE = 768
DEPTH = 512
SLOTS = 128
CHUNKS = 8
SPAN = STATIONS // CHUNKS
AHEAD = 5
CHIPS = 8
BLOCKS = 16
REGIONS = 16
FAR = 4
WHEN = (0, 2, 4, 6)
BUILDS = (5, 5, 5, 5, 6, 6)
PIECES = 8
PIECE = 256 // PIECES
MESH = pl.DeviceIdType.MESH


def when(condition):
    if isinstance(condition, bool):
        return lambda body: body() if condition else None
    return pl.when(condition)


def kernel(
    waves_ref, own_ref, number_ref, out_ref,
    bank, extra, last_tile, hankel, shifts, wave, halo_out, halo_in, scale_ref, corr, rows_ref, total,
    outgo, income, part, gathered,
    halo_sem, ring_send, ring_recv, share_send, share_recv, extra_send, extra_recv, extra_share,
    side_send, side_recv, spread_send, spread_recv,
):
    block = lax.axis_index("tmpl")
    region = lax.axis_index("sta")
    z = block // 2
    core = block % 2
    other = 1 - core

    def at(chip, which):
        return (lax.rem(chip + CHIPS, CHIPS) * 2 + which, region)

    barrier = pltpu.get_barrier_semaphore()
    near = [at(z, other), at(z + 1, core), at(z - 1, core), at(z + 2 * core - 1, other)]
    near += [(block, lax.rem(region + side, REGIONS)) for side in (1, REGIONS - 1)]
    for device in near:
        pl.semaphore_signal(barrier, inc=1, device_id=device, device_id_type=MESH)

    lane8 = lax.broadcasted_iota(jnp.int32, (CAP, 128), 1)
    coarse = waves_ref[...].astype(jnp.bfloat16)
    halo_out[...] = coarse[:, :256]
    for tile in range(4):
        wave[tile] = coarse[:, tile * 128 : tile * 128 + 128].astype(jnp.float32)

    last_tile[...] = jnp.zeros_like(last_tile)
    last_tile[:, : WINDOW - 384] = own_ref[:, 384:].astype(jnp.float32)
    for chunk in range(CHUNKS):
        rows = pl.ds(chunk * SPAN * CAP, SPAN * CAP)
        for tile in range(3):
            bank[block, chunk, pl.ds(tile * SPAN * CAP, SPAN * CAP), :] = own_ref[
                rows, tile * 128 : tile * 128 + 128
            ]
        ends = [last_tile[pl.ds((chunk * SPAN + i) * CAP, CAP), :] for i in range(SPAN)]
        joined = [
            jnp.where(lane8 < 64, ends[i], pltpu.roll(ends[i + 1], 64, 1)) for i in range(0, SPAN, 2)
        ]
        bank[block, chunk, pl.ds(3 * SPAN * CAP, SPAN * CAP // 2), :] = jnp.concatenate(
            joined, axis=0
        ).astype(jnp.bfloat16)
    spread_lane = lax.broadcasted_iota(jnp.int32, (STATIONS, 128), 1)
    spread_row = lax.broadcasted_iota(jnp.int32, (STATIONS, 128), 0)
    extras = jnp.zeros((CAP, 128), jnp.float32)
    for i, digits in enumerate((number_ref[...] >> 6, number_ref[...] & 63)):
        digits = digits.astype(jnp.float32).astype(jnp.bfloat16)
        selects = (spread_lane == spread_row * 4 + 2 + i).astype(jnp.bfloat16)
        extras = extras + jnp.dot(digits, selects, preferred_element_type=jnp.float32)
    for station in range(STATIONS):
        moved = pltpu.roll(last_tile[pl.ds(station * CAP, CAP), :], (station * 4 + 64) % 128, 1)
        extras = jnp.where((lane8 >> 1) == station * 2, moved, extras)
    extra[block] = jnp.concatenate([extras, jnp.zeros_like(extras)], axis=0).astype(jnp.bfloat16)
    pl.semaphore_wait(barrier, len(near))

    to_left = pltpu.make_async_remote_copy(
        src_ref=halo_out,
        dst_ref=halo_in,
        send_sem=halo_sem.at[0],
        recv_sem=halo_sem.at[1],
        device_id=(lax.rem(block + BLOCKS - 1, BLOCKS), region),
        device_id_type=MESH,
    )
    to_left.start()

    def index_of(chip):
        return lax.rem(chip + CHIPS, CHIPS) * 2 + core

    def remote(ref, send, receive, device):
        return pltpu.make_async_remote_copy(
            src_ref=ref, dst_ref=ref, send_sem=send, recv_sem=receive,
            device_id=device, device_id_type=MESH,
        )

    ahead = [at(z + 1, core), at(z - 1, core)]
    mate = at(z, other)

    def ring(way, chunk, hop, origin):
        ref = bank.at[index_of(origin), chunk]
        remote(ref, ring_send, ring_recv.at[chunk, hop], ahead[way]).start()

    def share(chunk, chip):
        remote(bank.at[index_of(chip), chunk], share_send, share_recv.at[chunk], mate).start()

    def ring_extra(way, hop, origin):
        remote(extra.at[index_of(origin)], extra_send, extra_recv.at[hop], ahead[way]).start()

    def share_extra(chip):
        remote(extra.at[index_of(chip)], extra_send, extra_share, mate).start()

    def inject(chunk):
        for way in range(2):
            ring(way, chunk, 0, z)
        share(chunk, z)

    for way in range(2):
        ring_extra(way, 0, z)
    for chunk in range(AHEAD + 1):
        inject(chunk)
    share_extra(z)

    total[...] = jnp.zeros_like(total)

    def waves_ready():
        to_left.wait()
        last = jnp.where(block == BLOCKS - 1, 0.0, 1.0)
        for tile in range(2):
            one = halo_in[:, tile * 128 : tile * 128 + 128]
            wave[4 + tile] = one.astype(jnp.float32) * last
        every = jnp.concatenate([wave[tile] for tile in range(6)], axis=1)
        for lane in range(16):
            moved = every if lane == 0 else pltpu.roll(every, WIDE - lane, 1)
            for tile in range(6):
                shifts[tile, pl.ds(lane, 96, stride=16), :] = moved[:, tile * 128 : tile * 128 + 128]
        pieces = []
        for tile in range(6):
            squared = jnp.zeros((STATIONS, 128), jnp.float32)
            for channel in range(3):
                one = wave[tile, pl.ds(channel * STATIONS, STATIONS), :]
                squared = squared + one * one
            pieces.append(squared)
        squared = jnp.concatenate(pieces, axis=1)
        def left(x, by):
            return pltpu.roll(x, WIDE - by, 1)
        two = squared + left(squared, 1)
        four = two + left(two, 2)
        run = four
        for by in (4, 8):
            run = run + left(run, by)
        sixteen = run
        for by in (16, 32, 64):
            run = run + left(run, by)
        run = run + left(sixteen, 128) + left(four, 144) + left(two, 148)
        scale_ref[...] = lax.rsqrt(run[:, :LAGS] / WINDOW + EPS)

    lower = lax.broadcasted_iota(jnp.int32, (16, LAGS), 0)

    def build(station):
        rolled, moved = [], {}
        for c in range(3):
            rows = pl.ds(pl.multiple_of((c * STATIONS + station) * 16, 16), 16)
            every = jnp.concatenate([shifts[tile, rows, :] for tile in range(6)], axis=1)
            rolled.append(every)

        def taken(channel, start):
            whole, lanes = divmod(start, 128)
            if (channel, lanes) not in moved:
                value = rolled[channel]
                moved[channel, lanes] = pltpu.roll(value, WIDE - lanes, 1) if lanes else value
            value = moved[channel, lanes]
            if whole < 0:
                return jnp.concatenate([value[:, WIDE - 128 :], value[:, : LAGS - 128]], axis=1)
            return value[:, whole * 128 : whole * 128 + LAGS]

        for tile in range(DEPTH // 16):
            first = tile * 16
            if first >= WINDOW:
                value = jnp.zeros((16, LAGS), jnp.float32)
            else:
                channel, start = divmod(first, TLEN)
                value = taken(channel, start)
                rest = TLEN - start
                if rest < 16:
                    if channel < 2:
                        after = taken(channel + 1, start - TLEN)
                    else:
                        after = jnp.zeros((16, LAGS), jnp.float32)
                    value = jnp.where(lower < rest, value, after)
            hankel[station, pl.ds(first, 16), :] = value.astype(jnp.bfloat16)

    ids = lax.broadcasted_iota(jnp.int32, (16, SLOTS), 1)
    picker = jnp.where(ids == WINDOW - 384, 64.0, jnp.where(ids == WINDOW + 1 - 384, 1.0, 0.0))
    picker = picker.astype(jnp.bfloat16)
    live = lax.broadcasted_iota(jnp.int32, (SLOTS, 128), 1) < WINDOW - 384

    lane_all = lax.broadcasted_iota(jnp.int32, (SLOTS, 128), 1)

    def correlate(chunk, pair, slot):
        tiles = []
        for tile in range(3):
            rows = pl.ds(pl.multiple_of(tile * SPAN * CAP + pair * 16, 16), 16)
            tiles.append([bank[b, chunk, rows, :].astype(jnp.float32) for b in range(BLOCKS)])
        rows = pl.ds(3 * SPAN * CAP, 16)
        ends = [bank[b, chunk, rows, :].astype(jnp.float32) for b in range(BLOCKS)]
        ends = jnp.concatenate([x[pair * 8 : pair * 8 + 8] for x in ends], axis=0)
        extras = jnp.concatenate([extra[b].astype(jnp.float32)[:8] for b in range(BLOCKS)], axis=0)
        for i in range(2):
            station = chunk * SPAN + pair * 2 + i
            end = ends if i == 0 else pltpu.roll(ends, 64, 1)
            few = pltpu.roll(extras, lax.rem(192 - station * 4, 128), 1)
            end = jnp.where(lane_all < 64, end, jnp.where(lane_all < 68, few, 0.0))
            pieces = [jnp.concatenate([x[i * 8 : i * 8 + 8] for x in t], axis=0) for t in tiles]
            one(station, slot, pair * 2 + i, jnp.concatenate(pieces + [end], axis=1))

    def one(station, slot, where, wide):
        waves = wide.astype(jnp.bfloat16)
        product = jnp.dot(waves, hankel[station], preferred_element_type=jnp.float32)
        last = jnp.where(live, wide[:, 384:], 0.0)
        power = last * last
        for tile in range(3):
            power = power + wide[:, tile * 128 : tile * 128 + 128] * wide[:, tile * 128 : tile * 128 + 128]
        power = jnp.sum(power, axis=1, keepdims=True)
        factor = lax.rsqrt(power / WINDOW + EPS) / WINDOW
        value = product * factor * scale_ref[pl.ds(station, 1), :]
        start = pl.multiple_of(where * SLOTS, SLOTS)
        corr[slot, pl.ds(start, SLOTS), :] = value.astype(jnp.bfloat16)
        row = lax.dot_general(
            picker, waves[:, 384:], (((1,), (1,)), ((), ())), preferred_element_type=jnp.float32
        )
        row = row[:8].astype(jnp.int32)
        group = row >> 8
        home = (row >> 4) & 15
        relative = (home - region + 1 + REGIONS) & 15
        apart = ((group >> 1) - z + CHIPS) & 7
        order = jnp.where(apart >= 4, 2 * apart - 8, 7 - 2 * apart)
        index = relative * 256 + (order * 2 + (group & 1)) * ROWS_DEV + (row & 15)
        index = jnp.where(row < 4096, index, 4096)
        rows_ref[slot, where] = index

    across = lax.broadcasted_iota(jnp.int32, (256, SLOTS), 0).astype(jnp.float32).astype(jnp.bfloat16)

    def scatter(relative, slot):
        picks = []
        for i in range(SPAN):
            index = rows_ref[slot, i] - relative * 256
            index = jnp.where((index >= 0) & (index < 256), index, 512)
            index = index.astype(jnp.float32).astype(jnp.bfloat16)
            same = across == jnp.broadcast_to(index[:1], (256, SLOTS))
            picks.append(jnp.where(same, jnp.bfloat16(1), jnp.bfloat16(0)))
        selector = jnp.concatenate(picks, axis=1)
        start = relative * 256
        total[pl.ds(start, 256), :] += jnp.dot(
            selector, corr[slot], preferred_element_type=jnp.float32
        )

    def moves(turn):
        for hop in range(FAR):
            chunk = turn - WHEN[hop]

            @when((chunk >= 0) & (chunk < CHUNKS))
            def _():
                odd = chunk % 2 if isinstance(chunk, int) else lax.rem(chunk, 2)
                count = 2 if hop < FAR - 1 else 1
                arrived = bank.at[0, pl.ds(0, count)]
                remote(arrived, ring_send, ring_recv.at[chunk, hop], mate).wait_recv()
                if hop == FAR - 1:
                    share(chunk, z + FAR)
                else:
                    origins = [z - hop - 1, z + hop + 1]
                    for way in range(2):

                        @when(True if hop + 1 < FAR - 1 else odd == way)
                        def _():
                            ring(way, chunk, hop + 1, origins[way])

                    for way in range(2):
                        share(chunk, origins[way])

            if isinstance(turn, int) and turn == WHEN[hop]:
                count = 2 if hop < FAR - 1 else 1
                arrived = extra.at[pl.ds(0, count)]
                remote(arrived, extra_send, extra_recv.at[hop], mate).wait_recv()
                if hop == FAR - 1:
                    share_extra(z + FAR)
                else:
                    for way in range(2):
                        origin = z + (-1 if way == 0 else 1) * (hop + 1)
                        if hop + 1 < FAR - 1 or way == 0:
                            ring_extra(way, hop + 1, origin)
                        share_extra(origin)

    def shared(chunk):
        remote(bank.at[pl.ds(0, CHIPS), 0], share_send, share_recv.at[chunk], mate).wait_recv()

    waves_ready()

    built = 0
    for turn in range(WHEN[-1]):
        moves(turn)
        if turn and turn + AHEAD < CHUNKS:
            inject(turn + AHEAD)
        many = BUILDS[turn]

        @pl.loop(built, built + many)
        def _(station):
            build(station)

        built += many

    def whole(chunk):
        slot = lax.rem(chunk, 2)
        scatter(0, slot)
        scatter(1, slot)
        scatter(2, slot)

    moves(WHEN[-1])
    remote(extra.at[pl.ds(0, CHIPS)], extra_send, extra_share, mate).wait_recv()
    shared(0)
    correlate(0, 0, 0)

    @pl.loop(1, CHUNKS - 1)
    def _(chunk):
        moves(WHEN[-1] + chunk)
        correlate(chunk - 1, 1, lax.rem(chunk + 1, 2))
        whole(chunk - 1)
        shared(chunk)
        correlate(chunk, 0, lax.rem(chunk, 2))

    moves(WHEN[-1] + CHUNKS - 1)
    correlate(CHUNKS - 2, 1, CHUNKS % 2)
    for relative in (0, 2):
        scatter(relative, CHUNKS % 2)
    shared(CHUNKS - 1)

    for pair in range(2):
        correlate(CHUNKS - 1, pair, 1 - CHUNKS % 2)

    def side(direction, piece):
        step = REGIONS - 1 if direction == 0 else 1
        span = pl.ds(piece * PIECE, PIECE)
        return pltpu.make_async_remote_copy(
            src_ref=outgo.at[direction, span],
            dst_ref=income.at[direction, span],
            send_sem=side_send.at[direction, piece],
            recv_sem=side_recv.at[direction, piece],
            device_id=(block, lax.rem(region + step, REGIONS)),
            device_id_type=MESH,
        )

    for direction in range(2):
        scatter(2 * direction, 1 - CHUNKS % 2)
        outgo[direction] = total[pl.ds(512 * direction, 256), :].astype(jnp.bfloat16)
        for piece in range(PIECES):
            side(direction, piece).start()
    scatter(1, CHUNKS % 2)
    scatter(1, 1 - CHUNKS % 2)

    def spread(piece, slot):
        order = piece * (CHIPS // PIECES) + slot // 2
        apart = 4 + order // 2 if order % 2 == 0 else 3 - order // 2
        return order, apart, slot % 2

    def send_out(order, apart, which):
        rows = pl.ds((order * 2 + which) * ROWS_DEV, ROWS_DEV)
        return pltpu.make_async_remote_copy(
            src_ref=part.at[rows],
            dst_ref=gathered.at[block],
            send_sem=spread_send.at[order * 2 + which],
            recv_sem=spread_recv.at[block],
            device_id=at(z + apart, which),
            device_id_type=MESH,
        )

    for piece in range(PIECES):
        for direction in range(2):
            side(direction, piece).wait_recv()
        span = pl.ds(piece * PIECE, PIECE)
        summed = total[pl.ds(256 + piece * PIECE, PIECE), :]
        summed = summed + income[0, span].astype(jnp.float32) + income[1, span].astype(jnp.float32)
        part[span] = summed.astype(jnp.bfloat16)
        for slot in range(BLOCKS // PIECES):
            order, apart, which = spread(piece, slot)
            if apart == 0:

                @pl.when(core != which)
                def _():
                    send_out(order, apart, which).start()

            else:
                send_out(order, apart, which).start()

    here = pl.ds(pl.multiple_of((14 + core) * ROWS_DEV, ROWS_DEV), ROWS_DEV)
    gathered[block] = part[here]

    remote(bank.at[pl.ds(0, 7)], ring_send, share_recv.at[0], mate).wait_send()
    remote(bank.at[pl.ds(0, 8)], share_send, share_recv.at[0], mate).wait_send()
    remote(extra.at[pl.ds(0, 15)], extra_send, extra_share, mate).wait_send()
    for direction in range(2):
        for piece in range(PIECES):
            side(direction, piece).wait_send()

    def spread_wait(source):
        return pltpu.make_async_remote_copy(
            src_ref=part.at[pl.ds(0, ROWS_DEV)],
            dst_ref=gathered.at[source],
            send_sem=spread_send.at[0],
            recv_sem=spread_recv.at[source],
            device_id=(block, region),
            device_id_type=MESH,
        )

    for piece in range(PIECES):
        for slot in range(BLOCKS // PIECES):
            order, apart, which = spread(piece, slot)
            if apart == 0:

                @pl.when(core != which)
                def _():
                    send_out(order, apart, which).wait_send()

            else:
                send_out(order, apart, which).wait_send()

    @pl.loop(1, BLOCKS)
    def _(step):
        spread_wait(lax.rem(block + step, BLOCKS)).wait_recv()

    for source in range(BLOCKS):
        out_ref[:, pl.ds(source * LAGS, LAGS)] = gathered[source]


def on_device(waveforms, templates, pair_rows):
    waves = waveforms.transpose(1, 0, 2).reshape(STATIONS * 3, LAGS)
    own = templates.reshape(STATIONS * CAP, WINDOW)
    bf16, f32 = jnp.bfloat16, jnp.float32
    dma = pltpu.SemaphoreType.DMA
    result = pl.pallas_call(
        kernel,
        out_shape=jax.ShapeDtypeStruct((ROWS_DEV, BLOCKS * LAGS), bf16),
        in_specs=[pl.BlockSpec(memory_space=pltpu.VMEM)] * 3,
        out_specs=pl.BlockSpec(memory_space=pltpu.VMEM),
        scratch_shapes=[
            pltpu.VMEM((BLOCKS, CHUNKS, 7 * SPAN * CAP // 2, 128), bf16),
            pltpu.VMEM((BLOCKS, 16, 128), bf16),
            pltpu.VMEM((STATIONS * CAP, 128), f32),
            pltpu.VMEM((STATIONS, DEPTH, LAGS), bf16),
            pltpu.VMEM((6, STATIONS * 3 * 16, 128), f32),
            pltpu.VMEM((6, STATIONS * 3, 128), f32),
            pltpu.VMEM((STATIONS * 3, 256), bf16),
            pltpu.VMEM((STATIONS * 3, 256), bf16),
            pltpu.VMEM((STATIONS, LAGS), f32),
            pltpu.VMEM((2, SPAN * SLOTS, LAGS), bf16),
            pltpu.VMEM((2, SPAN, 8, SLOTS), jnp.int32),
            pltpu.VMEM((768, LAGS), f32),
            pltpu.VMEM((2, 256, LAGS), bf16),
            pltpu.VMEM((2, 256, LAGS), bf16),
            pltpu.VMEM((256, LAGS), bf16),
            pltpu.VMEM((BLOCKS, ROWS_DEV, LAGS), bf16),
            dma((2,)),
            dma,
            dma((CHUNKS, FAR)),
            dma,
            dma((CHUNKS,)),
            dma,
            dma((FAR,)),
            dma,
            dma((2, PIECES)),
            dma((2, PIECES)),
            dma((BLOCKS,)),
            dma((BLOCKS,)),
        ],
        compiler_params=pltpu.CompilerParams(
            collective_id=0, has_side_effects=True, vmem_limit_bytes=60 * 1024 * 1024
        ),
    )(waves, own, pair_rows.T)
    return result.astype(jnp.float32)


def solution(mesh):
    in_specs = (P("sta", None, "tmpl"), P("sta", "tmpl", None), P("sta", "tmpl"))
    out_specs = P(("tmpl", "sta"), None)
    return jax.shard_map(
        on_device, mesh=mesh, in_specs=in_specs, out_specs=out_specs, check_vma=False
    )
```

```python
import functools

import jax
import jax.numpy as jnp
from jax import lax
from jax.experimental import pallas as pl
from jax.experimental.pallas import tpu as pltpu
from jax.sharding import PartitionSpec as P

TLEN = 150
WINDOW = 450
EPS = 1e-06
CAP = 8
ROWS_DEV = 16
STATIONS = 32
LAGS = 512
WIDE = 768
DEPTH = 512
SLOTS = 128
CHUNKS = 8
SPAN = STATIONS // CHUNKS
AHEAD = 3
CHIPS = 8
BLOCKS = 16
REGIONS = 16
FAR = 4
WHEN = (0, 2, 4, 6)
BUILDS = (4, 4, 6, 6, 6, 6)
PIECES = 8
PIECE = 256 // PIECES
MESH = pl.DeviceIdType.MESH


def when(condition):
    if isinstance(condition, bool):
        return lambda body: body() if condition else None
    return pl.when(condition)


def kernel(
    waves_ref, own_ref, number_ref, out_ref,
    bank, extra, last_tile, hankel, shifts, wave, halo_out, halo_in, scale_ref, corr, rows_ref, total,
    outgo, income, part, gathered,
    halo_sem, ring_send, ring_recv, share_send, share_recv, extra_send, extra_recv, extra_share,
    side_send, side_recv, spread_send, spread_recv,
):
    block = lax.axis_index("tmpl")
    region = lax.axis_index("sta")
    z = block // 2
    core = block % 2
    other = 1 - core

    def at(chip, which):
        return (lax.rem(chip + CHIPS, CHIPS) * 2 + which, region)

    barrier = pltpu.get_barrier_semaphore()
    near = [at(z, other), at(z + 1, core), at(z - 1, core), at(z + 2 * core - 1, other)]
    near += [(block, lax.rem(region + side, REGIONS)) for side in (1, REGIONS - 1)]
    for device in near:
        pl.semaphore_signal(barrier, inc=1, device_id=device, device_id_type=MESH)

    lane8 = lax.broadcasted_iota(jnp.int32, (CAP, 128), 1)
    coarse = waves_ref[...].astype(jnp.bfloat16)
    halo_out[...] = coarse[:, :256]
    for tile in range(4):
        wave[tile] = coarse[:, tile * 128 : tile * 128 + 128].astype(jnp.float32)

    last_tile[...] = jnp.zeros_like(last_tile)
    last_tile[:, : WINDOW - 384] = own_ref[:, 384:].astype(jnp.float32)
    for chunk in range(CHUNKS):
        rows = pl.ds(chunk * SPAN * CAP, SPAN * CAP)
        for tile in range(3):
            bank[block, chunk, pl.ds(tile * SPAN * CAP, SPAN * CAP), :] = own_ref[
                rows, tile * 128 : tile * 128 + 128
            ]
        ends = [last_tile[pl.ds((chunk * SPAN + i) * CAP, CAP), :] for i in range(SPAN)]
        joined = [
            jnp.where(lane8 < 64, ends[i], pltpu.roll(ends[i + 1], 64, 1)) for i in range(0, SPAN, 2)
        ]
        bank[block, chunk, pl.ds(3 * SPAN * CAP, SPAN * CAP // 2), :] = jnp.concatenate(
            joined, axis=0
        ).astype(jnp.bfloat16)
    spread_lane = lax.broadcasted_iota(jnp.int32, (STATIONS, 128), 1)
    spread_row = lax.broadcasted_iota(jnp.int32, (STATIONS, 128), 0)
    extras = jnp.zeros((CAP, 128), jnp.float32)
    for i, digits in enumerate((number_ref[...] >> 6, number_ref[...] & 63)):
        digits = digits.astype(jnp.float32).astype(jnp.bfloat16)
        selects = (spread_lane == spread_row * 4 + 2 + i).astype(jnp.bfloat16)
        extras = extras + jnp.dot(digits, selects, preferred_element_type=jnp.float32)
    for station in range(STATIONS):
        moved = pltpu.roll(last_tile[pl.ds(station * CAP, CAP), :], (station * 4 + 64) % 128, 1)
        extras = jnp.where((lane8 >> 1) == station * 2, moved, extras)
    extra[block] = jnp.concatenate([extras, jnp.zeros_like(extras)], axis=0).astype(jnp.bfloat16)
    pl.semaphore_wait(barrier, len(near))

    to_left = pltpu.make_async_remote_copy(
        src_ref=halo_out,
        dst_ref=halo_in,
        send_sem=halo_sem.at[0],
        recv_sem=halo_sem.at[1],
        device_id=(lax.rem(block + BLOCKS - 1, BLOCKS), region),
        device_id_type=MESH,
    )
    to_left.start()

    def index_of(chip):
        return lax.rem(chip + CHIPS, CHIPS) * 2 + core

    def remote(ref, send, receive, device):
        return pltpu.make_async_remote_copy(
            src_ref=ref, dst_ref=ref, send_sem=send, recv_sem=receive,
            device_id=device, device_id_type=MESH,
        )

    ahead = [at(z + 1, core), at(z - 1, core)]
    mate = at(z, other)

    def ring(way, chunk, hop, origin):
        ref = bank.at[index_of(origin), chunk]
        remote(ref, ring_send, ring_recv.at[chunk, hop], ahead[way]).start()

    def share(chunk, chip):
        remote(bank.at[index_of(chip), chunk], share_send, share_recv.at[chunk], mate).start()

    def ring_extra(way, hop, origin):
        remote(extra.at[index_of(origin)], extra_send, extra_recv.at[hop], ahead[way]).start()

    def share_extra(chip):
        remote(extra.at[index_of(chip)], extra_send, extra_share, mate).start()

    def inject(chunk):
        for way in range(2):
            ring(way, chunk, 0, z)
        share(chunk, z)

    for way in range(2):
        ring_extra(way, 0, z)
    for chunk in range(AHEAD + 1):
        inject(chunk)
    share_extra(z)

    total[...] = jnp.zeros_like(total)

    def waves_ready():
        to_left.wait()
        last = jnp.where(block == BLOCKS - 1, 0.0, 1.0)
        for tile in range(2):
            one = halo_in[:, tile * 128 : tile * 128 + 128]
            wave[4 + tile] = one.astype(jnp.float32) * last
        every = jnp.concatenate([wave[tile] for tile in range(6)], axis=1)
        for lane in range(16):
            moved = every if lane == 0 else pltpu.roll(every, WIDE - lane, 1)
            for tile in range(6):
                shifts[tile, pl.ds(lane, 96, stride=16), :] = moved[:, tile * 128 : tile * 128 + 128]
        pieces = []
        for tile in range(6):
            squared = jnp.zeros((STATIONS, 128), jnp.float32)
            for channel in range(3):
                one = wave[tile, pl.ds(channel * STATIONS, STATIONS), :]
                squared = squared + one * one
            pieces.append(squared)
        squared = jnp.concatenate(pieces, axis=1)
        def left(x, by):
            return pltpu.roll(x, WIDE - by, 1)
        two = squared + left(squared, 1)
        four = two + left(two, 2)
        run = four
        for by in (4, 8):
            run = run + left(run, by)
        sixteen = run
        for by in (16, 32, 64):
            run = run + left(run, by)
        run = run + left(sixteen, 128) + left(four, 144) + left(two, 148)
        scale_ref[...] = lax.rsqrt(run[:, :LAGS] / WINDOW + EPS)

    lower = lax.broadcasted_iota(jnp.int32, (16, LAGS), 0)

    def build(station):
        rolled, moved = [], {}
        for c in range(3):
            rows = pl.ds(pl.multiple_of((c * STATIONS + station) * 16, 16), 16)
            every = jnp.concatenate([shifts[tile, rows, :] for tile in range(6)], axis=1)
            rolled.append(every)

        def taken(channel, start):
            whole, lanes = divmod(start, 128)
            if (channel, lanes) not in moved:
                value = rolled[channel]
                moved[channel, lanes] = pltpu.roll(value, WIDE - lanes, 1) if lanes else value
            value = moved[channel, lanes]
            if whole < 0:
                return jnp.concatenate([value[:, WIDE - 128 :], value[:, : LAGS - 128]], axis=1)
            return value[:, whole * 128 : whole * 128 + LAGS]

        for tile in range(DEPTH // 16):
            first = tile * 16
            if first >= WINDOW:
                value = jnp.zeros((16, LAGS), jnp.float32)
            else:
                channel, start = divmod(first, TLEN)
                value = taken(channel, start)
                rest = TLEN - start
                if rest < 16:
                    if channel < 2:
                        after = taken(channel + 1, start - TLEN)
                    else:
                        after = jnp.zeros((16, LAGS), jnp.float32)
                    value = jnp.where(lower < rest, value, after)
            hankel[station, pl.ds(first, 16), :] = value.astype(jnp.bfloat16)

    ids = lax.broadcasted_iota(jnp.int32, (16, SLOTS), 1)
    picker = jnp.where(ids == WINDOW - 384, 64.0, jnp.where(ids == WINDOW + 1 - 384, 1.0, 0.0))
    picker = picker.astype(jnp.bfloat16)
    live = lax.broadcasted_iota(jnp.int32, (SLOTS, 128), 1) < WINDOW - 384

    lane_all = lax.broadcasted_iota(jnp.int32, (SLOTS, 128), 1)

    def correlate(chunk, pair, slot):
        tiles = []
        for tile in range(3):
            rows = pl.ds(pl.multiple_of(tile * SPAN * CAP + pair * 16, 16), 16)
            tiles.append([bank[b, chunk, rows, :].astype(jnp.float32) for b in range(BLOCKS)])
        rows = pl.ds(3 * SPAN * CAP, 16)
        ends = [bank[b, chunk, rows, :].astype(jnp.float32) for b in range(BLOCKS)]
        ends = jnp.concatenate([x[pair * 8 : pair * 8 + 8] for x in ends], axis=0)
        extras = jnp.concatenate([extra[b].astype(jnp.float32)[:8] for b in range(BLOCKS)], axis=0)
        for i in range(2):
            station = chunk * SPAN + pair * 2 + i
            end = ends if i == 0 else pltpu.roll(ends, 64, 1)
            few = pltpu.roll(extras, lax.rem(192 - station * 4, 128), 1)
            end = jnp.where(lane_all < 64, end, jnp.where(lane_all < 68, few, 0.0))
            pieces = [jnp.concatenate([x[i * 8 : i * 8 + 8] for x in t], axis=0) for t in tiles]
            one(station, slot, pair * 2 + i, jnp.concatenate(pieces + [end], axis=1))

    def one(station, slot, where, wide):
        waves = wide.astype(jnp.bfloat16)
        product = jnp.dot(waves, hankel[station], preferred_element_type=jnp.float32)
        last = jnp.where(live, wide[:, 384:], 0.0)
        power = last * last
        for tile in range(3):
            power = power + wide[:, tile * 128 : tile * 128 + 128] * wide[:, tile * 128 : tile * 128 + 128]
        power = jnp.sum(power, axis=1, keepdims=True)
        factor = lax.rsqrt(power / WINDOW + EPS) / WINDOW
        value = product * factor * scale_ref[pl.ds(station, 1), :]
        start = pl.multiple_of(where * SLOTS, SLOTS)
        corr[slot, pl.ds(start, SLOTS), :] = value.astype(jnp.bfloat16)
        row = lax.dot_general(
            picker, waves[:, 384:], (((1,), (1,)), ((), ())), preferred_element_type=jnp.float32
        )
        row = row[:8].astype(jnp.int32)
        group = row >> 8
        home = (row >> 4) & 15
        relative = (home - region + 1 + REGIONS) & 15
        apart = ((group >> 1) - z + CHIPS) & 7
        order = jnp.where(apart >= 4, 2 * apart - 8, 7 - 2 * apart)
        index = relative * 256 + (order * 2 + (group & 1)) * ROWS_DEV + (row & 15)
        index = jnp.where(row < 4096, index, 4096)
        rows_ref[slot, where] = index

    across = lax.broadcasted_iota(jnp.int32, (256, SLOTS), 0).astype(jnp.float32).astype(jnp.bfloat16)

    def scatter(relative, slot):
        picks = []
        for i in range(SPAN):
            index = rows_ref[slot, i] - relative * 256
            index = jnp.where((index >= 0) & (index < 256), index, 512)
            index = index.astype(jnp.float32).astype(jnp.bfloat16)
            same = across == jnp.broadcast_to(index[:1], (256, SLOTS))
            picks.append(jnp.where(same, jnp.bfloat16(1), jnp.bfloat16(0)))
        selector = jnp.concatenate(picks, axis=1)
        start = relative * 256
        total[pl.ds(start, 256), :] += jnp.dot(
            selector, corr[slot], preferred_element_type=jnp.float32
        )

    def moves(turn):
        for hop in range(FAR):
            chunk = turn - WHEN[hop]

            @when((chunk >= 0) & (chunk < CHUNKS))
            def _():
                odd = chunk % 2 if isinstance(chunk, int) else lax.rem(chunk, 2)
                count = 2 if hop < FAR - 1 else 1
                arrived = bank.at[0, pl.ds(0, count)]
                remote(arrived, ring_send, ring_recv.at[chunk, hop], mate).wait_recv()
                if hop == FAR - 1:
                    share(chunk, z + FAR)
                else:
                    origins = [z - hop - 1, z + hop + 1]
                    for way in range(2):

                        @when(True if hop + 1 < FAR - 1 else odd == way)
                        def _():
                            ring(way, chunk, hop + 1, origins[way])

                    for way in range(2):
                        share(chunk, origins[way])

            if isinstance(turn, int) and turn == WHEN[hop]:
                count = 2 if hop < FAR - 1 else 1
                arrived = extra.at[pl.ds(0, count)]
                remote(arrived, extra_send, extra_recv.at[hop], mate).wait_recv()
                if hop == FAR - 1:
                    share_extra(z + FAR)
                else:
                    for way in range(2):
                        origin = z + (-1 if way == 0 else 1) * (hop + 1)
                        if hop + 1 < FAR - 1 or way == 0:
                            ring_extra(way, hop + 1, origin)
                        share_extra(origin)

    def shared(chunk):
        remote(bank.at[pl.ds(0, CHIPS), 0], share_send, share_recv.at[chunk], mate).wait_recv()

    waves_ready()

    built = 0
    for turn in range(WHEN[-1]):
        moves(turn)
        if turn and turn + AHEAD < CHUNKS:
            inject(turn + AHEAD)
        many = BUILDS[turn]

        @pl.loop(built, built + many)
        def _(station):
            build(station)

        built += many

    def whole(chunk):
        slot = chunk % 2
        scatter(0, slot)
        scatter(1, slot)
        scatter(2, slot)

    moves(WHEN[-1])
    remote(extra.at[pl.ds(0, CHIPS)], extra_send, extra_share, mate).wait_recv()
    shared(0)
    correlate(0, 0, 0)

    for chunk in range(1, CHUNKS - 1):
        moves(WHEN[-1] + chunk)
        correlate(chunk - 1, 1, (chunk + 1) % 2)
        whole(chunk - 1)
        shared(chunk)
        correlate(chunk, 0, chunk % 2)

    moves(WHEN[-1] + CHUNKS - 1)
    correlate(CHUNKS - 2, 1, CHUNKS % 2)
    for relative in (0, 2):
        scatter(relative, CHUNKS % 2)
    shared(CHUNKS - 1)

    for pair in range(2):
        correlate(CHUNKS - 1, pair, 1 - CHUNKS % 2)

    def side(direction, piece):
        step = REGIONS - 1 if direction == 0 else 1
        span = pl.ds(piece * PIECE, PIECE)
        return pltpu.make_async_remote_copy(
            src_ref=outgo.at[direction, span],
            dst_ref=income.at[direction, span],
            send_sem=side_send.at[direction, piece],
            recv_sem=side_recv.at[direction, piece],
            device_id=(block, lax.rem(region + step, REGIONS)),
            device_id_type=MESH,
        )

    for direction in range(2):
        scatter(2 * direction, 1 - CHUNKS % 2)
        outgo[direction] = total[pl.ds(512 * direction, 256), :].astype(jnp.bfloat16)
        for piece in range(PIECES):
            side(direction, piece).start()
    scatter(1, CHUNKS % 2)
    scatter(1, 1 - CHUNKS % 2)

    def spread(piece, slot):
        order = piece * (CHIPS // PIECES) + slot // 2
        apart = 4 + order // 2 if order % 2 == 0 else 3 - order // 2
        return order, apart, slot % 2

    def send_out(order, apart, which):
        rows = pl.ds((order * 2 + which) * ROWS_DEV, ROWS_DEV)
        return pltpu.make_async_remote_copy(
            src_ref=part.at[rows],
            dst_ref=gathered.at[block],
            send_sem=spread_send.at[order * 2 + which],
            recv_sem=spread_recv.at[block],
            device_id=at(z + apart, which),
            device_id_type=MESH,
        )

    for piece in range(PIECES):
        for direction in range(2):
            side(direction, piece).wait_recv()
        span = pl.ds(piece * PIECE, PIECE)
        summed = total[pl.ds(256 + piece * PIECE, PIECE), :]
        summed = summed + income[0, span].astype(jnp.float32) + income[1, span].astype(jnp.float32)
        part[span] = summed.astype(jnp.bfloat16)
        for slot in range(BLOCKS // PIECES):
            order, apart, which = spread(piece, slot)
            if apart == 0:

                @pl.when(core != which)
                def _():
                    send_out(order, apart, which).start()

            else:
                send_out(order, apart, which).start()

    here = pl.ds(pl.multiple_of((14 + core) * ROWS_DEV, ROWS_DEV), ROWS_DEV)
    gathered[block] = part[here]

    remote(bank.at[pl.ds(0, 7)], ring_send, share_recv.at[0], mate).wait_send()
    remote(bank.at[pl.ds(0, 8)], share_send, share_recv.at[0], mate).wait_send()
    remote(extra.at[pl.ds(0, 15)], extra_send, extra_share, mate).wait_send()
    for direction in range(2):
        for piece in range(PIECES):
            side(direction, piece).wait_send()

    def spread_wait(source):
        return pltpu.make_async_remote_copy(
            src_ref=part.at[pl.ds(0, ROWS_DEV)],
            dst_ref=gathered.at[source],
            send_sem=spread_send.at[0],
            recv_sem=spread_recv.at[source],
            device_id=(block, region),
            device_id_type=MESH,
        )

    for piece in range(PIECES):
        for slot in range(BLOCKS // PIECES):
            order, apart, which = spread(piece, slot)
            if apart == 0:

                @pl.when(core != which)
                def _():
                    send_out(order, apart, which).wait_send()

            else:
                send_out(order, apart, which).wait_send()

    @pl.loop(1, BLOCKS)
    def _(step):
        spread_wait(lax.rem(block + step, BLOCKS)).wait_recv()

    for source in range(BLOCKS):
        out_ref[:, pl.ds(source * LAGS, LAGS)] = gathered[source]


def on_device(waveforms, templates, pair_rows):
    waves = waveforms.transpose(1, 0, 2).reshape(STATIONS * 3, LAGS)
    own = templates.reshape(STATIONS * CAP, WINDOW)
    bf16, f32 = jnp.bfloat16, jnp.float32
    dma = pltpu.SemaphoreType.DMA
    result = pl.pallas_call(
        kernel,
        out_shape=jax.ShapeDtypeStruct((ROWS_DEV, BLOCKS * LAGS), bf16),
        in_specs=[pl.BlockSpec(memory_space=pltpu.VMEM)] * 3,
        out_specs=pl.BlockSpec(memory_space=pltpu.VMEM),
        scratch_shapes=[
            pltpu.VMEM((BLOCKS, CHUNKS, 7 * SPAN * CAP // 2, 128), bf16),
            pltpu.VMEM((BLOCKS, 16, 128), bf16),
            pltpu.VMEM((STATIONS * CAP, 128), f32),
            pltpu.VMEM((STATIONS, DEPTH, LAGS), bf16),
            pltpu.VMEM((6, STATIONS * 3 * 16, 128), f32),
            pltpu.VMEM((6, STATIONS * 3, 128), f32),
            pltpu.VMEM((STATIONS * 3, 256), bf16),
            pltpu.VMEM((STATIONS * 3, 256), bf16),
            pltpu.VMEM((STATIONS, LAGS), f32),
            pltpu.VMEM((2, SPAN * SLOTS, LAGS), bf16),
            pltpu.VMEM((2, SPAN, 8, SLOTS), jnp.int32),
            pltpu.VMEM((768, LAGS), f32),
            pltpu.VMEM((2, 256, LAGS), bf16),
            pltpu.VMEM((2, 256, LAGS), bf16),
            pltpu.VMEM((256, LAGS), bf16),
            pltpu.VMEM((BLOCKS, ROWS_DEV, LAGS), bf16),
            dma((2,)),
            dma,
            dma((CHUNKS, FAR)),
            dma,
            dma((CHUNKS,)),
            dma,
            dma((FAR,)),
            dma,
            dma((2, PIECES)),
            dma((2, PIECES)),
            dma((BLOCKS,)),
            dma((BLOCKS,)),
        ],
        compiler_params=pltpu.CompilerParams(
            collective_id=0, has_side_effects=True, vmem_limit_bytes=60 * 1024 * 1024
        ),
    )(waves, own, pair_rows.T)
    return result.astype(jnp.float32)


def solution(mesh):
    in_specs = (P("sta", None, "tmpl"), P("sta", "tmpl", None), P("sta", "tmpl"))
    out_specs = P(("tmpl", "sta"), None)
    return jax.shard_map(
        on_device, mesh=mesh, in_specs=in_specs, out_specs=out_specs, check_vma=False
    )
```

```python
import functools

import jax
import jax.numpy as jnp
from jax import lax
from jax.experimental import pallas as pl
from jax.experimental.pallas import tpu as pltpu
from jax.sharding import PartitionSpec as P

TLEN = 150
WINDOW = 450
EPS = 1e-06
CAP = 8
ROWS_DEV = 16
STATIONS = 32
LAGS = 512
WIDE = 768
DEPTH = 512
SLOTS = 128
CHUNKS = 8
SPAN = STATIONS // CHUNKS
AHEAD = 3
CHIPS = 8
BLOCKS = 16
REGIONS = 16
FAR = 4
WHEN = (0, 2, 4, 6)
BUILDS = (4, 4, 6, 6, 6, 6)
PIECES = 8
PIECE = 256 // PIECES
MESH = pl.DeviceIdType.MESH


def when(condition):
    if isinstance(condition, bool):
        return lambda body: body() if condition else None
    return pl.when(condition)


def kernel(
    waves_ref, own_ref, number_ref, out_ref,
    bank, extra, last_tile, hankel, shifts, wave, halo_out, halo_in, scale_ref, corr, rows_ref, total,
    outgo, income, part, gathered,
    halo_sem, ring_send, ring_recv, share_send, share_recv, extra_send, extra_recv, extra_share,
    side_send, side_recv, spread_send, spread_recv,
):
    block = lax.axis_index("tmpl")
    region = lax.axis_index("sta")
    z = block // 2
    core = block % 2
    other = 1 - core

    def at(chip, which):
        return (lax.rem(chip + CHIPS, CHIPS) * 2 + which, region)

    barrier = pltpu.get_barrier_semaphore()
    near = [at(z, other), at(z + 1, core), at(z - 1, core), at(z + 2 * core - 1, other)]
    near += [(block, lax.rem(region + side, REGIONS)) for side in (1, REGIONS - 1)]
    for device in near:
        pl.semaphore_signal(barrier, inc=1, device_id=device, device_id_type=MESH)

    lane8 = lax.broadcasted_iota(jnp.int32, (CAP, 128), 1)
    coarse = waves_ref[...].astype(jnp.bfloat16)
    halo_out[...] = coarse[:, :256]
    for tile in range(4):
        wave[tile] = coarse[:, tile * 128 : tile * 128 + 128].astype(jnp.float32)

    last_tile[...] = jnp.zeros_like(last_tile)
    last_tile[:, : WINDOW - 384] = own_ref[:, 384:].astype(jnp.float32)
    for chunk in range(CHUNKS):
        rows = pl.ds(chunk * SPAN * CAP, SPAN * CAP)
        for tile in range(3):
            bank[block, chunk, pl.ds(tile * SPAN * CAP, SPAN * CAP), :] = own_ref[
                rows, tile * 128 : tile * 128 + 128
            ]
        ends = [last_tile[pl.ds((chunk * SPAN + i) * CAP, CAP), :] for i in range(SPAN)]
        joined = [
            jnp.where(lane8 < 64, ends[i], pltpu.roll(ends[i + 1], 64, 1)) for i in range(0, SPAN, 2)
        ]
        bank[block, chunk, pl.ds(3 * SPAN * CAP, SPAN * CAP // 2), :] = jnp.concatenate(
            joined, axis=0
        ).astype(jnp.bfloat16)
    spread_lane = lax.broadcasted_iota(jnp.int32, (STATIONS, 128), 1)
    spread_row = lax.broadcasted_iota(jnp.int32, (STATIONS, 128), 0)
    extras = jnp.zeros((CAP, 128), jnp.float32)
    for i, digits in enumerate((number_ref[...] >> 6, number_ref[...] & 63)):
        digits = digits.astype(jnp.float32).astype(jnp.bfloat16)
        selects = (spread_lane == spread_row * 4 + 2 + i).astype(jnp.bfloat16)
        extras = extras + jnp.dot(digits, selects, preferred_element_type=jnp.float32)
    for station in range(STATIONS):
        moved = pltpu.roll(last_tile[pl.ds(station * CAP, CAP), :], (station * 4 + 64) % 128, 1)
        extras = jnp.where((lane8 >> 1) == station * 2, moved, extras)
    extra[block] = jnp.concatenate([extras, jnp.zeros_like(extras)], axis=0).astype(jnp.bfloat16)
    pl.semaphore_wait(barrier, len(near))

    to_left = pltpu.make_async_remote_copy(
        src_ref=halo_out,
        dst_ref=halo_in,
        send_sem=halo_sem.at[0],
        recv_sem=halo_sem.at[1],
        device_id=(lax.rem(block + BLOCKS - 1, BLOCKS), region),
        device_id_type=MESH,
    )
    to_left.start()

    def index_of(chip):
        return lax.rem(chip + CHIPS, CHIPS) * 2 + core

    def remote(ref, send, receive, device):
        return pltpu.make_async_remote_copy(
            src_ref=ref, dst_ref=ref, send_sem=send, recv_sem=receive,
            device_id=device, device_id_type=MESH,
        )

    ahead = [at(z + 1, core), at(z - 1, core)]
    mate = at(z, other)

    def ring(way, chunk, hop, origin):
        ref = bank.at[index_of(origin), chunk]
        remote(ref, ring_send, ring_recv.at[chunk, hop], ahead[way]).start()

    def share(chunk, chip):
        remote(bank.at[index_of(chip), chunk], share_send, share_recv.at[chunk], mate).start()

    def ring_extra(way, hop, origin):
        remote(extra.at[index_of(origin)], extra_send, extra_recv.at[hop], ahead[way]).start()

    def share_extra(chip):
        remote(extra.at[index_of(chip)], extra_send, extra_share, mate).start()

    def inject(chunk):
        for way in range(2):
            ring(way, chunk, 0, z)
        share(chunk, z)

    for way in range(2):
        ring_extra(way, 0, z)
    for chunk in range(AHEAD + 1):
        inject(chunk)
    share_extra(z)

    total[...] = jnp.zeros_like(total)

    def waves_ready():
        to_left.wait()
        last = jnp.where(block == BLOCKS - 1, 0.0, 1.0)
        for tile in range(2):
            one = halo_in[:, tile * 128 : tile * 128 + 128]
            wave[4 + tile] = one.astype(jnp.float32) * last
        every = jnp.concatenate([wave[tile] for tile in range(6)], axis=1)
        for lane in range(16):
            moved = every if lane == 0 else pltpu.roll(every, WIDE - lane, 1)
            for tile in range(6):
                shifts[tile, pl.ds(lane, 96, stride=16), :] = moved[:, tile * 128 : tile * 128 + 128]
        pieces = []
        for tile in range(6):
            squared = jnp.zeros((STATIONS, 128), jnp.float32)
            for channel in range(3):
                one = wave[tile, pl.ds(channel * STATIONS, STATIONS), :]
                squared = squared + one * one
            pieces.append(squared)
        squared = jnp.concatenate(pieces, axis=1)
        def left(x, by):
            return pltpu.roll(x, WIDE - by, 1)
        two = squared + left(squared, 1)
        four = two + left(two, 2)
        run = four
        for by in (4, 8):
            run = run + left(run, by)
        sixteen = run
        for by in (16, 32, 64):
            run = run + left(run, by)
        run = run + left(sixteen, 128) + left(four, 144) + left(two, 148)
        scale_ref[...] = lax.rsqrt(run[:, :LAGS] / WINDOW + EPS)

    lower = lax.broadcasted_iota(jnp.int32, (16, LAGS), 0)

    def build(station):
        rolled, moved = [], {}
        for c in range(3):
            rows = pl.ds(pl.multiple_of((c * STATIONS + station) * 16, 16), 16)
            every = jnp.concatenate([shifts[tile, rows, :] for tile in range(6)], axis=1)
            rolled.append(every)

        def taken(channel, start):
            whole, lanes = divmod(start, 128)
            if (channel, lanes) not in moved:
                value = rolled[channel]
                moved[channel, lanes] = pltpu.roll(value, WIDE - lanes, 1) if lanes else value
            value = moved[channel, lanes]
            if whole < 0:
                return jnp.concatenate([value[:, WIDE - 128 :], value[:, : LAGS - 128]], axis=1)
            return value[:, whole * 128 : whole * 128 + LAGS]

        for tile in range(DEPTH // 16):
            first = tile * 16
            if first >= WINDOW:
                value = jnp.zeros((16, LAGS), jnp.float32)
            else:
                channel, start = divmod(first, TLEN)
                value = taken(channel, start)
                rest = TLEN - start
                if rest < 16:
                    if channel < 2:
                        after = taken(channel + 1, start - TLEN)
                    else:
                        after = jnp.zeros((16, LAGS), jnp.float32)
                    value = jnp.where(lower < rest, value, after)
            hankel[station, pl.ds(first, 16), :] = value.astype(jnp.bfloat16)

    ids = lax.broadcasted_iota(jnp.int32, (16, SLOTS), 1)
    picker = jnp.where(ids == WINDOW - 384, 64.0, jnp.where(ids == WINDOW + 1 - 384, 1.0, 0.0))
    picker = picker.astype(jnp.bfloat16)
    live = lax.broadcasted_iota(jnp.int32, (SLOTS, 128), 1) < WINDOW - 384

    lane_all = lax.broadcasted_iota(jnp.int32, (SLOTS, 128), 1)

    def correlate(chunk, pair, slot):
        tiles = []
        for tile in range(3):
            rows = pl.ds(pl.multiple_of(tile * SPAN * CAP + pair * 16, 16), 16)
            tiles.append([bank[b, chunk, rows, :].astype(jnp.float32) for b in range(BLOCKS)])
        rows = pl.ds(3 * SPAN * CAP, 16)
        ends = [bank[b, chunk, rows, :].astype(jnp.float32) for b in range(BLOCKS)]
        ends = jnp.concatenate([x[pair * 8 : pair * 8 + 8] for x in ends], axis=0)
        extras = jnp.concatenate([extra[b].astype(jnp.float32)[:8] for b in range(BLOCKS)], axis=0)
        for i in range(2):
            station = chunk * SPAN + pair * 2 + i
            end = ends if i == 0 else pltpu.roll(ends, 64, 1)
            few = pltpu.roll(extras, lax.rem(192 - station * 4, 128), 1)
            end = jnp.where(lane_all < 64, end, jnp.where(lane_all < 68, few, 0.0))
            pieces = [jnp.concatenate([x[i * 8 : i * 8 + 8] for x in t], axis=0) for t in tiles]
            one(station, slot, pair * 2 + i, jnp.concatenate(pieces + [end], axis=1))

    def one(station, slot, where, wide):
        waves = wide.astype(jnp.bfloat16)
        product = jnp.dot(waves, hankel[station], preferred_element_type=jnp.float32)
        last = jnp.where(live, wide[:, 384:], 0.0)
        power = last * last
        for tile in range(3):
            power = power + wide[:, tile * 128 : tile * 128 + 128] * wide[:, tile * 128 : tile * 128 + 128]
        power = jnp.sum(power, axis=1, keepdims=True)
        factor = lax.rsqrt(power / WINDOW + EPS) / WINDOW
        value = product * factor * scale_ref[pl.ds(station, 1), :]
        start = pl.multiple_of(where * SLOTS, SLOTS)
        corr[slot, pl.ds(start, SLOTS), :] = value.astype(jnp.bfloat16)
        row = lax.dot_general(
            picker, waves[:, 384:], (((1,), (1,)), ((), ())), preferred_element_type=jnp.float32
        )
        row = row[:8].astype(jnp.int32)
        group = row >> 8
        home = (row >> 4) & 15
        relative = (home - region + 1 + REGIONS) & 15
        apart = ((group >> 1) - z + CHIPS) & 7
        order = jnp.where(apart >= 4, 2 * apart - 8, 7 - 2 * apart)
        index = relative * 256 + (order * 2 + (group & 1)) * ROWS_DEV + (row & 15)
        index = jnp.where(row < 4096, index, 4096)
        rows_ref[slot, where] = index

    across = lax.broadcasted_iota(jnp.int32, (256, SLOTS), 0).astype(jnp.float32).astype(jnp.bfloat16)

    def scatter(relative, slot):
        picks = []
        for i in range(SPAN):
            index = rows_ref[slot, i] - relative * 256
            index = jnp.where((index >= 0) & (index < 256), index, 512)
            index = index.astype(jnp.float32).astype(jnp.bfloat16)
            same = across == jnp.broadcast_to(index[:1], (256, SLOTS))
            picks.append(jnp.where(same, jnp.bfloat16(1), jnp.bfloat16(0)))
        selector = jnp.concatenate(picks, axis=1)
        start = relative * 256
        total[pl.ds(start, 256), :] += jnp.dot(
            selector, corr[slot], preferred_element_type=jnp.float32
        )

    def moves(turn):
        for hop in range(FAR):
            chunk = turn - WHEN[hop]

            @when((chunk >= 0) & (chunk < CHUNKS))
            def _():
                odd = chunk % 2 if isinstance(chunk, int) else lax.rem(chunk, 2)
                count = 2 if hop < FAR - 1 else 1
                arrived = bank.at[0, pl.ds(0, count)]
                remote(arrived, ring_send, ring_recv.at[chunk, hop], mate).wait_recv()
                if hop == FAR - 1:
                    share(chunk, z + FAR)
                else:
                    origins = [z - hop - 1, z + hop + 1]
                    for way in range(2):

                        @when(True if hop + 1 < FAR - 1 else odd == way)
                        def _():
                            ring(way, chunk, hop + 1, origins[way])

                    for way in range(2):
                        share(chunk, origins[way])

            if isinstance(turn, int) and turn == WHEN[hop]:
                count = 2 if hop < FAR - 1 else 1
                arrived = extra.at[pl.ds(0, count)]
                remote(arrived, extra_send, extra_recv.at[hop], mate).wait_recv()
                if hop == FAR - 1:
                    share_extra(z + FAR)
                else:
                    for way in range(2):
                        origin = z + (-1 if way == 0 else 1) * (hop + 1)
                        if hop + 1 < FAR - 1 or way == 0:
                            ring_extra(way, hop + 1, origin)
                        share_extra(origin)

    def shared(chunk):
        remote(bank.at[pl.ds(0, CHIPS), 0], share_send, share_recv.at[chunk], mate).wait_recv()

    waves_ready()

    built = 0
    for turn in range(WHEN[-1]):
        moves(turn)
        if turn and turn + AHEAD < CHUNKS:
            inject(turn + AHEAD)
        many = BUILDS[turn]

        @pl.loop(built, built + many)
        def _(station):
            build(station)

        built += many

    def whole(chunk):
        slot = chunk % 2
        scatter(0, slot)
        scatter(1, slot)
        scatter(2, slot)

    moves(WHEN[-1])
    remote(extra.at[pl.ds(0, CHIPS)], extra_send, extra_share, mate).wait_recv()
    shared(0)
    correlate(0, 0, 0)

    for chunk in range(1, CHUNKS - 1):
        moves(WHEN[-1] + chunk)
        correlate(chunk - 1, 1, (chunk + 1) % 2)
        whole(chunk - 1)
        shared(chunk)
        correlate(chunk, 0, chunk % 2)

    moves(WHEN[-1] + CHUNKS - 1)
    correlate(CHUNKS - 2, 1, CHUNKS % 2)
    for relative in (0, 2):
        scatter(relative, CHUNKS % 2)
    shared(CHUNKS - 1)

    for pair in range(2):
        correlate(CHUNKS - 1, pair, 1 - CHUNKS % 2)

    def side(direction, piece):
        step = REGIONS - 1 if direction == 0 else 1
        span = pl.ds(piece * PIECE, PIECE)
        return pltpu.make_async_remote_copy(
            src_ref=outgo.at[direction, span],
            dst_ref=income.at[direction, span],
            send_sem=side_send.at[direction, piece],
            recv_sem=side_recv.at[direction, piece],
            device_id=(block, lax.rem(region + step, REGIONS)),
            device_id_type=MESH,
        )

    for direction in range(2):
        scatter(2 * direction, 1 - CHUNKS % 2)
        outgo[direction] = total[pl.ds(512 * direction, 256), :].astype(jnp.bfloat16)
        for piece in range(PIECES):
            side(direction, piece).start()
    scatter(1, CHUNKS % 2)
    scatter(1, 1 - CHUNKS % 2)

    def spread(piece, slot):
        order = piece * (CHIPS // PIECES) + slot // 2
        apart = 4 + order // 2 if order % 2 == 0 else 3 - order // 2
        return order, apart, slot % 2

    def send_out(order, apart, which):
        rows = pl.ds((order * 2 + which) * ROWS_DEV, ROWS_DEV)
        return pltpu.make_async_remote_copy(
            src_ref=part.at[rows],
            dst_ref=gathered.at[block],
            send_sem=spread_send.at[order * 2 + which],
            recv_sem=spread_recv.at[block],
            device_id=at(z + apart, which),
            device_id_type=MESH,
        )

    for piece in range(PIECES):
        for direction in range(2):
            side(direction, piece).wait_recv()
        span = pl.ds(piece * PIECE, PIECE)
        summed = total[pl.ds(256 + piece * PIECE, PIECE), :]
        summed = summed + income[0, span].astype(jnp.float32) + income[1, span].astype(jnp.float32)
        part[span] = summed.astype(jnp.bfloat16)
        for slot in range(BLOCKS // PIECES):
            order, apart, which = spread(piece, slot)
            if apart == 0:

                @pl.when(core != which)
                def _():
                    send_out(order, apart, which).start()

            else:
                send_out(order, apart, which).start()

    here = pl.ds(pl.multiple_of((14 + core) * ROWS_DEV, ROWS_DEV), ROWS_DEV)
    gathered[block] = part[here]

    remote(bank.at[pl.ds(0, 7)], ring_send, share_recv.at[0], mate).wait_send()
    remote(bank.at[pl.ds(0, 8)], share_send, share_recv.at[0], mate).wait_send()
    remote(extra.at[pl.ds(0, 15)], extra_send, extra_share, mate).wait_send()
    for direction in range(2):
        for piece in range(PIECES):
            side(direction, piece).wait_send()

    def spread_wait(source):
        return pltpu.make_async_remote_copy(
            src_ref=part.at[pl.ds(0, ROWS_DEV)],
            dst_ref=gathered.at[source],
            send_sem=spread_send.at[0],
            recv_sem=spread_recv.at[source],
            device_id=(block, region),
            device_id_type=MESH,
        )

    for piece in range(PIECES):
        for slot in range(BLOCKS // PIECES):
            order, apart, which = spread(piece, slot)
            if apart == 0:

                @pl.when(core != which)
                def _():
                    send_out(order, apart, which).wait_send()

            else:
                send_out(order, apart, which).wait_send()

    @pl.loop(1, BLOCKS)
    def _(step):
        spread_wait(lax.rem(block + step, BLOCKS)).wait_recv()

    for source in range(BLOCKS):
        out_ref[:, pl.ds(source * LAGS, LAGS)] = gathered[source]


def widen(narrow_ref, wide_ref):
    wide_ref[...] = narrow_ref[...].astype(jnp.float32)


def on_device(waveforms, templates, pair_rows):
    waves = waveforms.transpose(1, 0, 2).reshape(STATIONS * 3, LAGS)
    own = templates.reshape(STATIONS * CAP, WINDOW)
    bf16, f32 = jnp.bfloat16, jnp.float32
    dma = pltpu.SemaphoreType.DMA
    result = pl.pallas_call(
        kernel,
        out_shape=jax.ShapeDtypeStruct((ROWS_DEV, BLOCKS * LAGS), bf16),
        in_specs=[pl.BlockSpec(memory_space=pltpu.VMEM)] * 3,
        out_specs=pl.BlockSpec(memory_space=pltpu.VMEM),
        scratch_shapes=[
            pltpu.VMEM((BLOCKS, CHUNKS, 7 * SPAN * CAP // 2, 128), bf16),
            pltpu.VMEM((BLOCKS, 16, 128), bf16),
            pltpu.VMEM((STATIONS * CAP, 128), f32),
            pltpu.VMEM((STATIONS, DEPTH, LAGS), bf16),
            pltpu.VMEM((6, STATIONS * 3 * 16, 128), f32),
            pltpu.VMEM((6, STATIONS * 3, 128), f32),
            pltpu.VMEM((STATIONS * 3, 256), bf16),
            pltpu.VMEM((STATIONS * 3, 256), bf16),
            pltpu.VMEM((STATIONS, LAGS), f32),
            pltpu.VMEM((2, SPAN * SLOTS, LAGS), bf16),
            pltpu.VMEM((2, SPAN, 8, SLOTS), jnp.int32),
            pltpu.VMEM((768, LAGS), f32),
            pltpu.VMEM((2, 256, LAGS), bf16),
            pltpu.VMEM((2, 256, LAGS), bf16),
            pltpu.VMEM((256, LAGS), bf16),
            pltpu.VMEM((BLOCKS, ROWS_DEV, LAGS), bf16),
            dma((2,)),
            dma,
            dma((CHUNKS, FAR)),
            dma,
            dma((CHUNKS,)),
            dma,
            dma((FAR,)),
            dma,
            dma((2, PIECES)),
            dma((2, PIECES)),
            dma((BLOCKS,)),
            dma((BLOCKS,)),
        ],
        compiler_params=pltpu.CompilerParams(
            collective_id=0, has_side_effects=True, vmem_limit_bytes=60 * 1024 * 1024
        ),
    )(waves, own, pair_rows.T)
    return pl.pallas_call(
        widen,
        out_shape=jax.ShapeDtypeStruct((ROWS_DEV, BLOCKS * LAGS), f32),
        in_specs=[pl.BlockSpec(memory_space=pltpu.VMEM)],
        out_specs=pl.BlockSpec(memory_space=pltpu.VMEM),
    )(result)


def solution(mesh):
    in_specs = (P("sta", None, "tmpl"), P("sta", "tmpl", None), P("sta", "tmpl"))
    out_specs = P(("tmpl", "sta"), None)
    return jax.shard_map(
        on_device, mesh=mesh, in_specs=in_specs, out_specs=out_specs, check_vma=False
    )
```
